128 devices in a mesh: ctx: 64 (over x, y, z_hi, core), head: 2 (over z_lo).
Axes of the slice: x: 4, y: 4, z: 4 (z_hi: 2, z_lo: 2; z = z_hi * 2 + z_lo), core: 2. Of those that a mesh axis runs over, the one named last changes fastest.
Arguments:
- content_rows: bfloat16 [4, 512, 4, 2048], P(None, 'ctx'), may hold values from -6 to 6
- w_hidden: bfloat16 [2048, 4096], P(None, 'head'), may hold values from -0.125 to 0.125
- w_embed: bfloat16 [4096, 512], P('head'), may hold values from -0.09375 to 0.09375
- w_query: bfloat16 [512, 512], P(None, 'head'), may hold values from -0.25 to 0.25
- w_gate: bfloat16 [512, 512], P(None, 'head'), may hold values from -0.25 to 0.25
- w_proj: bfloat16 [512, 512], P('head'), may hold values from -0.25 to 0.25
- history_keys: bfloat16 [4, 147456, 512], P(None, 'ctx', 'head'), may hold values from -6 to 6
- history_values: bfloat16 [4, 147456, 512], P(None, 'ctx', 'head'), may hold values from -6 to 6
- cutoffs: int32 [4, 512], replicated, may hold values from 36864 to 147456
- out_cotangent: bfloat16 [4, 512, 512], P(None, 'ctx'), may hold values from -6 to 6
Outputs:
- content_grad: bfloat16 [4, 512, 4, 2048], P(None, 'ctx', 'head')
The draws below stay inside these ranges and needn't reach their ends.
Inputs may be any that keep to these rules, and one draw needn't show every extreme that they name: cutoffs[u, t] counts the leading events of user u's history that its target t sees.
All inputs are finite; a program needn't handle non-finite values.
Results may differ from the reference program's by a relative error of at most 0.02.
Values may be sent and summed in bfloat16 or wider, within the bound.
A program may use at most 128 MiB of HBM per device.

```python
import jax
import jax.numpy as jnp
from jax import lax

D = 512
HEADS = 4
DH = 128
CONTENT = 2048
MLP_HID = 4096
CONTENT_ROWS = 4
USERS = 4
EV_DEV = 2304
TGT_USER = 512
HIST_LEN = 147456


def place_ends(values, key, low, high):
    longest = values.shape.index(max(values.shape))
    spots = []
    for shift in (0, 1):
        where = [jax.random.randint(jax.random.fold_in(key, axis), (), 0, length) for axis, length in enumerate(values.shape)]
        where[longest] = (where[longest] + shift) % values.shape[longest]
        spots.append(tuple(where))
    return values.at[spots[0]].set(low).at[spots[1]].set(high)


def block_levels(rng, shape, split, least, largest):
    def one(dim, parts):
        steps = jax.random.uniform(jax.random.fold_in(jax.random.fold_in(rng, 6), dim), (parts,), jnp.float32, least / len(split), largest / len(split))
        return jnp.repeat(jnp.exp(steps), shape[dim] // parts).reshape((-1,) + (1,) * (len(shape) - dim - 1))

    level = one(*split[0])
    for cut in split[1:]:
        level = level * one(*cut)
    return level


def scatter_about(rng, shape, spread, reach, pieces=(), kind=jnp.bfloat16):
    drawn = spread * jax.random.normal(rng, shape, jnp.float32)
    if pieces:
        drawn = drawn * block_levels(rng, shape, pieces, -0.22, 0.18)
    return jnp.clip(drawn, -reach, reach).astype(kind)


def setup_inputs(seed: int = 0) -> dict:
    keys = jax.random.split(jax.random.key(seed), 11)
    content_rows = scatter_about(keys[0], (USERS, TGT_USER, CONTENT_ROWS, CONTENT), 1.0, 6.0, ((1, 64),))
    w_hidden = scatter_about(keys[1], (CONTENT, MLP_HID), CONTENT ** -0.5, 0.125, ((1, 2),))
    w_embed = scatter_about(keys[2], (MLP_HID, D), MLP_HID ** -0.5, 0.09375, ((0, 2),))
    w_query = scatter_about(keys[3], (D, D), D ** -0.5, 0.25, ((1, 2),))
    w_gate = scatter_about(keys[4], (D, D), D ** -0.5, 0.25, ((1, 2),))
    w_proj = scatter_about(keys[5], (D, D), D ** -0.5, 0.25, ((0, 2),))
    history_keys = scatter_about(keys[6], (USERS, HIST_LEN, D), 1.0, 6.0, ((1, 64), (2, 2)))
    history_values = scatter_about(keys[7], (USERS, HIST_LEN, D), 1.0, 6.0, ((1, 64), (2, 2)))
    cutoffs = place_ends(jax.random.randint(keys[8], (USERS, TGT_USER), HIST_LEN // 4, HIST_LEN + 1), jax.random.fold_in(keys[8], 1), HIST_LEN // 4, HIST_LEN).astype(jnp.int32)
    out_cotangent = scatter_about(keys[9], (USERS, TGT_USER, D), 1.0, 6.0, ((1, 64),))
    return {"content_rows": content_rows, "w_hidden": w_hidden, "w_embed": w_embed, "w_query": w_query, "w_gate": w_gate, "w_proj": w_proj, "history_keys": history_keys, "history_values": history_values, "cutoffs": cutoffs, "out_cotangent": out_cotangent}


def silu_slope(values_in):
    sigmoid_part = jax.nn.sigmoid(values_in)
    return sigmoid_part * (1.0 + values_in * (1.0 - sigmoid_part))

def contract_last(left, right):
    return lax.dot_general(left, right, (((1,), (1,)), ((), ())), preferred_element_type=jnp.float32)

def reference(content_rows, w_hidden, w_embed, w_query, w_gate, w_proj, history_keys, history_values, cutoffs, out_cotangent):
    flat_rows = content_rows.reshape(-1, CONTENT)
    hidden_lin = jnp.dot(flat_rows, w_hidden, preferred_element_type=jnp.float32)
    hidden = jax.nn.silu(hidden_lin).astype(jnp.bfloat16)
    encoded = jnp.dot(hidden, w_embed, preferred_element_type=jnp.float32)
    encoded = encoded.reshape(USERS * TGT_USER, CONTENT_ROWS, D)
    embedded = (0.5 * lax.optimization_barrier(jnp.sum(encoded, axis=1))).astype(jnp.bfloat16)
    query_lin = jnp.dot(embedded, w_query, preferred_element_type=jnp.float32)
    gate_lin = jnp.dot(embedded, w_gate, preferred_element_type=jnp.float32)
    queries = jax.nn.silu(query_lin).astype(jnp.bfloat16).reshape(USERS, TGT_USER, HEADS, DH)
    gates = jax.nn.silu(gate_lin).astype(jnp.bfloat16)
    out_grad = contract_last(out_cotangent.reshape(-1, D), w_proj).astype(jnp.bfloat16)
    score_scale = DH ** (-0.5)
    blocks = HIST_LEN // EV_DEV
    starts = jnp.arange(blocks, dtype=jnp.int32) * EV_DEV
    key_heads = history_keys.reshape(USERS, blocks, EV_DEV, HEADS, DH)
    value_heads = history_values.reshape(USERS, blocks, EV_DEV, HEADS, DH)

    def forward_user(packed):
        user_queries, limits, user_keys, user_values = packed
        query_float = user_queries.astype(jnp.float32)

        def block_step(total, inputs):
            block_keys, block_values, start = inputs
            scores = jnp.einsum('thd,phd->htp', query_float, block_keys.astype(jnp.float32)) * score_scale
            positions = start + jnp.arange(EV_DEV, dtype=jnp.int32)
            visible = positions[None, :] < limits[:, None]
            weights = jnp.where(visible[None], jax.nn.silu(scores), 0.0).astype(jnp.bfloat16)
            return (total + jnp.einsum('htp,phd->thd', weights.astype(jnp.float32), block_values.astype(jnp.float32)), None)
        begin = jnp.zeros((TGT_USER, HEADS, DH), jnp.float32)
        total, unused = lax.scan(block_step, begin, (user_keys, user_values, starts))
        return total
    attended = lax.map(forward_user, (queries, cutoffs, key_heads, value_heads))
    rscale = lax.rsqrt(lax.optimization_barrier(jnp.mean(attended * attended, axis=-1, keepdims=True)) + 1e-06)
    normed = attended * rscale
    grad_heads = out_grad.reshape(USERS, TGT_USER, HEADS, DH).astype(jnp.float32)
    gate_heads = gates.reshape(USERS, TGT_USER, HEADS, DH).astype(jnp.float32)
    gate_grad = grad_heads * normed
    normed_grad = grad_heads * gate_heads
    attn_grad = (rscale * (normed_grad - normed * lax.optimization_barrier(jnp.mean(normed_grad * normed, axis=-1, keepdims=True)))).astype(jnp.bfloat16)

    def backward_user(packed):
        user_queries, limits, user_keys, user_values, user_grads = packed
        query_float = user_queries.astype(jnp.float32)
        grad_float = user_grads.astype(jnp.float32)

        def block_step(total, inputs):
            block_keys, block_values, start = inputs
            keys_float = block_keys.astype(jnp.float32)
            scores = jnp.einsum('thd,phd->htp', query_float, keys_float) * score_scale
            positions = start + jnp.arange(EV_DEV, dtype=jnp.int32)
            visible = positions[None, :] < limits[:, None]
            weight_grad = jnp.einsum('thd,phd->htp', grad_float, block_values.astype(jnp.float32))
            grad_scores = jnp.where(visible[None], weight_grad * silu_slope(scores), 0.0).astype(jnp.bfloat16)
            return (total + jnp.einsum('htp,phd->thd', grad_scores.astype(jnp.float32), keys_float), None)
        begin = jnp.zeros((TGT_USER, HEADS, DH), jnp.float32)
        total, unused = lax.scan(block_step, begin, (user_keys, user_values, starts))
        return total * score_scale
    query_grad = lax.map(backward_user, (queries, cutoffs, key_heads, value_heads, attn_grad))
    query_back = (query_grad.reshape(-1, D) * silu_slope(query_lin)).astype(jnp.bfloat16)
    gate_back = (gate_grad.reshape(-1, D) * silu_slope(gate_lin)).astype(jnp.bfloat16)
    embed_total = contract_last(query_back, w_query) + contract_last(gate_back, w_gate)
    embed_grad = (0.5 * embed_total).astype(jnp.bfloat16)
    hidden_grad = contract_last(embed_grad, w_embed)
    slopes = silu_slope(hidden_lin).reshape(USERS * TGT_USER, CONTENT_ROWS, MLP_HID)
    hidden_back = (hidden_grad[:, None, :] * slopes).astype(jnp.bfloat16).reshape(-1, MLP_HID)
    content_grad = contract_last(hidden_back, w_hidden).astype(jnp.bfloat16)
    return content_grad.reshape(USERS, TGT_USER, CONTENT_ROWS, CONTENT)
```

```python
import jax
import jax.numpy as jnp
from jax import lax
from jax.experimental import pallas as pl
from jax.experimental.pallas import tpu as pltpu
from jax.sharding import Mesh
from jax.sharding import PartitionSpec as P

DH = 128
CTX = ("x", "y", "zh", "c")
BF = jnp.bfloat16
F32 = jnp.float32
LAST = (((1,), (1,)), ((), ()))
USERS, ROWS, EACH, WIDTH = 4, 8, 4, 2048
HALF, MODEL, LOCAL = 2048, 512, 256
TARGETS, EVENTS = 512, 2304
OWN = USERS * ROWS
CUT_ROWS = 128
HID_CHUNKS = 4
HID_CHUNK = HALF // HID_CHUNKS
OUT_CHUNKS = 4
OUT_CHUNK = WIDTH // OUT_CHUNKS
SCALE = DH**-0.5


def contract_last(left, right):
    return lax.dot_general(left, right, LAST, preferred_element_type=F32)


def dot(left, right):
    return jnp.dot(left, right, preferred_element_type=F32)


def silu(v):
    return v * jax.nn.sigmoid(v)


def silu_slope(v):
    s = jax.nn.sigmoid(v)
    return s * (1.0 + v * (1.0 - s))


def kernel(
    x_hbm, wh_hbm, we_hbm, wq_hbm, wg_hbm, wp_hbm, k_hbm, v_hbm, cut_hbm, cot_hbm,
    out_ref,
    x_v, wh_v, we_v, wq_v, wg_v, wp_v, k_v, v_v, cut_v, cot_v,
    slope_v, hid_slope, enc_send, enc_recv, lin_q, lin_g, gates_v, outg_v, gateg_v, qgrad_v,
    ag1, ag2, rs1_send, rs1_recv, rs2_send, rs2_recv,
    emb_send, emb_recv, part_send, part_recv, part_own,
    load_sem, kv_sem, ag_ssem, ag_rsem, rs_ssem, rs_rsem, head_ssem, head_rsem,
):
    xi, yi, zi, ci, hi = (lax.axis_index(a) for a in (*CTX, "head"))
    i1 = yi * 2 + ci
    i2 = xi * 2 + zi
    base = (((xi * 4 + yi) * 2 + zi) * 2 + ci) * EVENTS
    partner = {"head": 1 - hi}

    def id1(p):
        return {"y": p // 2, "c": lax.rem(p, 2)}

    def id2(p):
        return {"x": p // 2, "zh": lax.rem(p, 2)}

    barrier = pltpu.get_barrier_semaphore()
    pl.semaphore_signal(barrier, inc=1, device_id=partner, device_id_type=pl.DeviceIdType.MESH)
    for k in range(1, 8):
        for me, ids in ((i1, id1), (i2, id2)):
            pl.semaphore_signal(
                barrier, inc=1, device_id=ids(lax.rem(me + k, 8)),
                device_id_type=pl.DeviceIdType.MESH,
            )

    loads = [pltpu.make_async_copy(x_hbm, x_v, load_sem.at[0])]
    for j in range(HID_CHUNKS):
        cols = pl.ds(j * HID_CHUNK, HID_CHUNK)
        loads.append(
            pltpu.make_async_copy(wh_hbm.at[:, cols], wh_v.at[:, cols], load_sem.at[len(loads)])
        )
    for src, dst in (
        (we_hbm, we_v), (cot_hbm, cot_v), (wp_hbm, wp_v), (wq_hbm, wq_v), (wg_hbm, wg_v),
        (cut_hbm, cut_v),
    ):
        loads.append(pltpu.make_async_copy(src, dst, load_sem.at[len(loads)]))
    for copy in loads:
        copy.start()

    def kv_copies(u):
        return (
            pltpu.make_async_copy(k_hbm.at[u], k_v.at[u], kv_sem.at[0, u]),
            pltpu.make_async_copy(v_hbm.at[u], v_v.at[u], kv_sem.at[1, u]),
        )

    for u in range(USERS):
        for copy in kv_copies(u):
            copy.start()

    loads[0].wait()
    for j in range(HID_CHUNKS):
        loads[1 + j].wait()
        cols = slice(j * HID_CHUNK, (j + 1) * HID_CHUNK)
        lin = dot(x_v[...], wh_v[:, cols])
        s = jax.nn.sigmoid(lin)
        hidden = lin * s
        hid_slope[:, cols] = s * (1.0 + lin * (1.0 - s))
        if j == 0:
            loads[1 + HID_CHUNKS].wait()
        part = dot(hidden.astype(BF), we_v[cols, :])
        total = part if j == 0 else total + part
    enc_send[...] = total[0:32] + total[32:64] + total[64:96] + total[96:128]

    pl.semaphore_wait(barrier, 15)

    def head_copy(src, dst, n):
        return pltpu.make_async_remote_copy(
            src_ref=src, dst_ref=dst, send_sem=head_ssem.at[n], recv_sem=head_rsem.at[n],
            device_id=partner, device_id_type=pl.DeviceIdType.MESH,
        )

    enc_copy = head_copy(enc_send, enc_recv, 0)
    enc_copy.start()
    for n in range(2 + HID_CHUNKS, 7 + HID_CHUNKS):
        loads[n].wait()
    cot = cot_v[...].astype(F32).reshape(OWN, MODEL).astype(BF)
    outg_v[...] = contract_last(cot, wp_v[...]).astype(BF).astype(F32)
    enc_copy.wait()
    embedded = (0.5 * (enc_send[...] + enc_recv[...])).astype(BF)
    query_lin = dot(embedded, wq_v[...])
    lin_q[...] = silu_slope(query_lin)
    queries = silu(query_lin).astype(BF).astype(F32)

    def send_seven(src, dst, ssem, rsem, me, ids):
        for k in range(1, 8):
            peer = lax.rem(me + k, 8)
            pltpu.make_async_remote_copy(
                src_ref=src(peer), dst_ref=dst, send_sem=ssem, recv_sem=rsem,
                device_id=ids(peer), device_id_type=pl.DeviceIdType.MESH,
            ).start()

    def seven(ref, ssem, rsem):
        return pltpu.make_async_remote_copy(
            src_ref=ref, dst_ref=ref, send_sem=ssem, recv_sem=rsem,
            device_id=partner, device_id_type=pl.DeviceIdType.MESH,
        )

    def gather_first(ph, u, block):
        rows = pl.ds(pl.multiple_of(i2 * ROWS, ROWS), ROWS)
        ag1[ph, u, rows, :] = block
        ref = ag1.at[ph, u, rows, :]
        send_seven(lambda p: ref, ref, ag_ssem.at[ph, u, 0], ag_rsem.at[ph, u, 0], i2, id2)

    def gather_second(ph, u):
        seven(ag1.at[ph, u, 0:56, :], ag_ssem.at[ph, u, 0], ag_rsem.at[ph, u, 0]).wait_recv()
        rows = pl.ds(pl.multiple_of(i1 * 64, 64), 64)
        ag2[ph, u, rows, :] = ag1[ph, u].astype(BF)
        ref = ag2.at[ph, u, rows, :]
        send_seven(lambda p: ref, ref, ag_ssem.at[ph, u, 1], ag_rsem.at[ph, u, 1], i1, id1)

    def gather_end(ph, u):
        seven(ag2.at[ph, u, 0:448, :], ag_ssem.at[ph, u, 1], ag_rsem.at[ph, u, 1]).wait_recv()

    def sum_first(ph, u):
        mine = pl.ds(pl.multiple_of(i1 * 64, 64), 64)
        rs1_recv[ph, u, mine, :] = rs1_send[ph, u, mine, :]
        send_seven(
            lambda p: rs1_send.at[ph, u, pl.ds(pl.multiple_of(p * 64, 64), 64), :],
            rs1_recv.at[ph, u, mine, :],
            rs_ssem.at[ph, u, 0], rs_rsem.at[ph, u, 0], i1, id1,
        )

    def sum_second(ph, u):
        seven(rs1_recv.at[ph, u, 0:448, :], rs_ssem.at[ph, u, 0], rs_rsem.at[ph, u, 0]).wait_recv()
        total = rs1_recv[ph, u, 0:64, :].astype(F32)
        for g in range(1, 8):
            total = total + rs1_recv[ph, u, g * 64 : (g + 1) * 64, :].astype(F32)
        rs2_send[ph, u] = total
        mine = pl.ds(pl.multiple_of(i2 * ROWS, ROWS), ROWS)
        rs2_recv[ph, u, mine, :] = rs2_send[ph, u, mine, :]
        send_seven(
            lambda p: rs2_send.at[ph, u, pl.ds(pl.multiple_of(p * ROWS, ROWS), ROWS), :],
            rs2_recv.at[ph, u, mine, :],
            rs_ssem.at[ph, u, 1], rs_rsem.at[ph, u, 1], i2, id2,
        )

    def sum_end(ph, u):
        seven(rs2_recv.at[ph, u, 0:56, :], rs_ssem.at[ph, u, 1], rs_rsem.at[ph, u, 1]).wait_recv()
        total = rs2_recv[ph, u, 0:8, :]
        for g in range(1, 8):
            total = total + rs2_recv[ph, u, g * 8 : (g + 1) * 8, :]
        return total

    for u in range(USERS):
        gather_first(0, u, queries[u * ROWS : (u + 1) * ROWS])
    gate_lin = dot(embedded, wg_v[...])
    lin_g[...] = silu_slope(gate_lin)
    gates_v[...] = silu(gate_lin).astype(BF).astype(F32)
    for u in range(USERS):
        gather_second(0, u)

    def own_rows(u):
        return pl.ds(pl.multiple_of(u * ROWS, ROWS), ROWS)

    def norm_and_gather(u):
        attended = sum_end(0, u)
        rows = own_rows(u)
        grads = outg_v[rows, :]
        gates = gates_v[rows, :]
        blocks, gate_blocks = [], []
        for h in range(2):
            cols = slice(h * DH, (h + 1) * DH)
            a, g, gate = attended[:, cols], grads[:, cols], gates[:, cols]
            rscale = lax.rsqrt(jnp.mean(a * a, axis=-1, keepdims=True) + 1e-06)
            normed = a * rscale
            gate_blocks.append(g * normed)
            ng = g * gate
            grad = rscale * (ng - normed * jnp.mean(ng * normed, axis=-1, keepdims=True))
            blocks.append(grad.astype(BF).astype(F32))
        gateg_v[rows, :] = jnp.concatenate(gate_blocks, axis=1)
        gather_first(1, u, jnp.concatenate(blocks, axis=1))

    def query_grad_end(u):
        qgrad_v[own_rows(u), :] = sum_end(1, u) * SCALE

    lane = lax.broadcasted_iota(jnp.int32, (1, EVENTS), 1) + base

    def forward(u, h):
        cols = pl.ds(pl.multiple_of(h * DH, DH), DH)
        for r in range(0, TARGETS, CUT_ROWS):
            rows = slice(r, r + CUT_ROWS)
            scores = contract_last(ag2[0, u, rows, cols], k_v[u, :, cols])
            cut = cut_v[u, rows, :]
            visible = lane < jnp.concatenate([cut] * (EVENTS // DH), axis=1)
            y = jnp.where(visible, scores * (0.5 * SCALE), -1e30).astype(BF)
            t = jnp.tanh(y)
            s2 = BF(1) + t
            w = y * s2
            slope_v[u * 2 + h, rows, :] = BF(0.5) * s2 + w * (BF(0.5) - BF(0.5) * t)
            rs1_send[0, u, rows, cols] = dot(w, v_v[u, :, cols]).astype(BF)

    def backward(u, h):
        cols = pl.ds(pl.multiple_of(h * DH, DH), DH)
        for r in range(0, TARGETS, CUT_ROWS):
            rows = slice(r, r + CUT_ROWS)
            wgrad = contract_last(ag2[1, u, rows, cols], v_v[u, :, cols])
            gs = wgrad.astype(BF) * slope_v[u * 2 + h, rows, :]
            rs1_send[1, u, rows, cols] = dot(gs, k_v[u, :, cols]).astype(BF)

    @pl.loop(0, 2 * USERS)
    def _(i):
        u = i // 2
        h = lax.rem(i, 2)

        @pl.when(h == 0)
        def _():
            gather_end(0, u)
            for copy in kv_copies(u):
                copy.wait()

        forward(u, h)

        @pl.when(h == 1)
        def _():
            sum_first(0, u)

            @pl.when(u >= 1)
            def _():
                norm_and_gather(u - 1)

        @pl.when((h == 0) & (u >= 1))
        def _():
            sum_second(0, u - 1)

            @pl.when(u >= 2)
            def _():
                gather_second(1, u - 2)

    @pl.loop(0, 2 * USERS)
    def _(i):
        u = i // 2
        h = lax.rem(i, 2)

        @pl.when(h == 0)
        def _():
            gather_end(1, u)

        backward(u, h)

        @pl.when(h == 1)
        def _():
            sum_first(1, u)

        @pl.when(i == 0)
        def _():
            sum_second(0, USERS - 1)
            gather_second(1, USERS - 2)

        @pl.when(i == 1)
        def _():
            norm_and_gather(USERS - 1)

        @pl.when(i == 2)
        def _():
            gather_second(1, USERS - 1)

        @pl.when((h == 0) & (u >= 1))
        def _():
            sum_second(1, u - 1)

        @pl.when((h == 1) & (u >= 1))
        def _():
            query_grad_end(u - 1)

    sum_second(1, USERS - 1)
    query_grad_end(USERS - 1)

    query_back = (qgrad_v[...] * lin_q[...]).astype(BF)
    gate_back = (gateg_v[...] * lin_g[...]).astype(BF)
    emb_send[...] = (
        contract_last(query_back, wq_v[...]) + contract_last(gate_back, wg_v[...])
    ).astype(BF)
    emb_copy = head_copy(emb_send, emb_recv, 1)
    emb_copy.start()
    emb_copy.wait()
    embed_grad = (0.5 * (emb_send[...].astype(F32) + emb_recv[...].astype(F32))).astype(BF)
    hidden_grad = contract_last(embed_grad, we_v[...])
    hidden_back = jnp.concatenate(
        [(hidden_grad * hid_slope[r * OWN : (r + 1) * OWN, :]).astype(BF) for r in range(EACH)],
        axis=0,
    )
    x_v[...] = hidden_back
    mine = pl.ds(pl.multiple_of(hi * 64, 64), 64)
    other = pl.ds(pl.multiple_of((1 - hi) * 64, 64), 64)
    copies = []
    for j in range(OUT_CHUNKS):
        cols = slice(j * OUT_CHUNK, (j + 1) * OUT_CHUNK)
        part_own[:, cols] = contract_last(x_v[...], wh_v[cols, :])
        part_send[j] = part_own[other, cols].astype(BF)
        copies.append(head_copy(part_send.at[j], part_recv.at[j], 2 + j))
        copies[-1].start()
    for j in range(OUT_CHUNKS):
        cols = slice(j * OUT_CHUNK, (j + 1) * OUT_CHUNK)
        copies[j].wait()
        own = part_own[mine, cols].astype(BF).astype(F32)
        out_ref[:, cols] = (own + part_recv[j].astype(F32)).astype(BF)

    @pl.loop(0, USERS)
    def _(u):
        for ph in range(2):
            seven(ag1.at[ph, u, 0:56, :], ag_ssem.at[ph, u, 0], ag_rsem.at[ph, u, 0]).wait_send()
            seven(ag2.at[ph, u, 0:448, :], ag_ssem.at[ph, u, 1], ag_rsem.at[ph, u, 1]).wait_send()
            seven(rs1_send.at[ph, u, 0:448, :], rs_ssem.at[ph, u, 0], rs_rsem.at[ph, u, 0]).wait_send()
            seven(rs2_send.at[ph, u, 0:56, :], rs_ssem.at[ph, u, 1], rs_rsem.at[ph, u, 1]).wait_send()


def body(
    content_rows, w_hidden, w_embed, w_query, w_gate, w_proj,
    history_keys, history_values, cutoffs, out_cotangent,
):
    x = content_rows.transpose(2, 0, 1, 3).reshape(EACH * OWN, WIDTH)
    cut = cutoffs.reshape(USERS, 4, 4, 2, 2, ROWS).transpose(0, 2, 4, 1, 3, 5)
    cut = jnp.broadcast_to(cut.reshape(USERS, TARGETS, 1), (USERS, TARGETS, DH))
    dma = pltpu.SemaphoreType.DMA
    v = pltpu.VMEM
    part = pl.pallas_call(
        kernel,
        name="attention_and_encoder",
        out_shape=jax.ShapeDtypeStruct((64, WIDTH), BF),
        in_specs=[pl.BlockSpec(memory_space=pl.ANY)] * 10,
        out_specs=pl.BlockSpec(memory_space=pltpu.VMEM),
        scratch_shapes=[
            v((EACH * OWN, WIDTH), BF), v((WIDTH, HALF), BF), v((HALF, MODEL), BF),
            v((MODEL, LOCAL), BF), v((MODEL, LOCAL), BF), v((LOCAL, MODEL), BF),
            v((USERS, EVENTS, LOCAL), BF), v((USERS, EVENTS, LOCAL), BF),
            v((USERS, TARGETS, DH), jnp.int32), v((USERS, ROWS, MODEL), BF),
            v((2 * USERS, TARGETS, EVENTS), BF), v((EACH * OWN, HALF), F32),
            v((OWN, MODEL), F32), v((OWN, MODEL), F32),
            v((OWN, LOCAL), F32), v((OWN, LOCAL), F32), v((OWN, LOCAL), F32),
            v((OWN, LOCAL), F32), v((OWN, LOCAL), F32), v((OWN, LOCAL), F32),
            v((2, USERS, 64, LOCAL), F32), v((2, USERS, TARGETS, LOCAL), BF),
            v((2, USERS, TARGETS, LOCAL), BF), v((2, USERS, TARGETS, LOCAL), BF),
            v((2, USERS, 64, LOCAL), F32), v((2, USERS, 64, LOCAL), F32),
            v((OWN, MODEL), BF), v((OWN, MODEL), BF),
            v((OUT_CHUNKS, 64, OUT_CHUNK), BF), v((OUT_CHUNKS, 64, OUT_CHUNK), BF),
            v((EACH * OWN, WIDTH), F32),
            dma((7 + HID_CHUNKS,)), dma((2, USERS)),
            dma((2, USERS, 2)), dma((2, USERS, 2)), dma((2, USERS, 2)), dma((2, USERS, 2)),
            dma((2 + OUT_CHUNKS,)), dma((2 + OUT_CHUNKS,)),
        ],
        compiler_params=pltpu.CompilerParams(
            collective_id=0, has_side_effects=True, vmem_limit_bytes=62 * 2**20
        ),
    )(
        x, w_hidden, w_embed, w_query, w_gate, w_proj,
        history_keys, history_values, cut, out_cotangent,
    )
    return part.reshape(2, USERS, ROWS, WIDTH).transpose(1, 2, 0, 3)


def solution(mesh):
    split = Mesh(
        mesh.devices.reshape(4, 4, 2, 2, mesh.shape["head"]),
        (*CTX, "head"),
    )
    return jax.shard_map(
        body,
        mesh=split,
        in_specs=(
            P(None, CTX, None, None), P(None, "head"), P("head", None), P(None, "head"),
            P(None, "head"), P("head", None), P(None, CTX, "head"), P(None, CTX, "head"),
            P(), P(None, CTX, None),
        ),
        out_specs=P(None, CTX, "head", None),
        check_vma=False,
    )
```

```python
import jax
import jax.numpy as jnp
from jax import lax
from jax.experimental import pallas as pl
from jax.experimental.pallas import tpu as pltpu
from jax.sharding import Mesh
from jax.sharding import PartitionSpec as P

DH = 128
CTX = ("x", "y", "zh", "c")
BF = jnp.bfloat16
F32 = jnp.float32
LAST = (((1,), (1,)), ((), ()))
USERS, ROWS, EACH, WIDTH = 4, 8, 4, 2048
HALF, MODEL, LOCAL = 2048, 512, 256
TARGETS, EVENTS = 512, 2304
OWN = USERS * ROWS
SLOTS, NEAR = 64, 32
OFFSETS = sorted(
    [(a, b, c) for a in range(4) for b in range(4) for c in range(2) if a or b or c],
    key=lambda t: -(min(t[0], 4 - t[0]) + min(t[1], 4 - t[1]) + 2 * t[2]),
)
CUT_ROWS = 128
HID_CHUNKS = 4
HID_CHUNK = HALF // HID_CHUNKS
OUT_CHUNKS = 4
OUT_CHUNK = WIDTH // OUT_CHUNKS
SCALE = DH**-0.5


def contract_last(left, right):
    return lax.dot_general(left, right, LAST, preferred_element_type=F32)


def dot(left, right):
    return jnp.dot(left, right, preferred_element_type=F32)


def silu(v):
    return v * jax.nn.sigmoid(v)


def silu_slope(v):
    s = jax.nn.sigmoid(v)
    return s * (1.0 + v * (1.0 - s))


def kernel(
    x_hbm, wh_hbm, we_hbm, wq_hbm, wg_hbm, wp_hbm, k_hbm, v_hbm, cut_hbm, cot_hbm,
    out_ref,
    x_v, wh_v, we_v, wq_v, wg_v, wp_v, k_v, v_v, cut_v, cot_v,
    slope_v, hid_slope, enc_send, enc_recv, lin_q, lin_g, gates_v, outg_v, gateg_v, qgrad_v,
    ag, rows_v, sums_v, rs1_send, rs1_recv, rs2_send, rs2_recv,
    emb_send, emb_recv, part_send, part_recv, part_own,
    load_sem, kv_sem, ag_ssem, ag_rsem, rs_ssem, rs_rsem, head_ssem, head_rsem,
):
    xi, yi, zi, ci, hi = (lax.axis_index(a) for a in (*CTX, "head"))
    base = (((xi * 4 + yi) * 2 + zi) * 2 + ci) * EVENTS
    partner = {"head": 1 - hi}
    sibling = {"c": 1 - ci}

    spot = (xi * 4 + yi) * 2 + zi
    peers = []
    for dx, dy, dz in OFFSETS:
        px, py, pz = lax.rem(xi + dx, 4), lax.rem(yi + dy, 4), lax.rem(zi + dz, 2)
        peers.append(((px * 4 + py) * 2 + pz, {"x": px, "y": py, "zh": pz}))

    barrier = pltpu.get_barrier_semaphore()
    for device in [partner, sibling] + [device for _, device in peers]:
        pl.semaphore_signal(barrier, inc=1, device_id=device, device_id_type=pl.DeviceIdType.MESH)

    loads = [pltpu.make_async_copy(x_hbm, x_v, load_sem.at[0])]
    for j in range(HID_CHUNKS):
        cols = pl.ds(j * HID_CHUNK, HID_CHUNK)
        loads.append(
            pltpu.make_async_copy(wh_hbm.at[:, cols], wh_v.at[:, cols], load_sem.at[len(loads)])
        )
    for src, dst in (
        (we_hbm, we_v), (cot_hbm, cot_v), (wp_hbm, wp_v), (wq_hbm, wq_v), (wg_hbm, wg_v),
        (cut_hbm, cut_v),
    ):
        loads.append(pltpu.make_async_copy(src, dst, load_sem.at[len(loads)]))
    for copy in loads:
        copy.start()

    def kv_copies(u):
        return (
            pltpu.make_async_copy(k_hbm.at[u], k_v.at[u], kv_sem.at[0, u]),
            pltpu.make_async_copy(v_hbm.at[u], v_v.at[u], kv_sem.at[1, u]),
        )

    for u in range(USERS):
        for copy in kv_copies(u):
            copy.start()

    loads[0].wait()
    for j in range(HID_CHUNKS):
        loads[1 + j].wait()
        cols = slice(j * HID_CHUNK, (j + 1) * HID_CHUNK)
        lin = dot(x_v[...], wh_v[:, cols])
        s = jax.nn.sigmoid(lin)
        hidden = lin * s
        hid_slope[:, cols] = s * (1.0 + lin * (1.0 - s))
        if j == 0:
            loads[1 + HID_CHUNKS].wait()
        part = dot(hidden.astype(BF), we_v[cols, :])
        total = part if j == 0 else total + part
    enc_send[...] = total[0:32] + total[32:64] + total[64:96] + total[96:128]

    pl.semaphore_wait(barrier, 33)

    def head_copy(src, dst, n):
        return pltpu.make_async_remote_copy(
            src_ref=src, dst_ref=dst, send_sem=head_ssem.at[n], recv_sem=head_rsem.at[n],
            device_id=partner, device_id_type=pl.DeviceIdType.MESH,
        )

    enc_copy = head_copy(enc_send, enc_recv, 0)
    enc_copy.start()
    for n in range(2 + HID_CHUNKS, 7 + HID_CHUNKS):
        loads[n].wait()
    cot = cot_v[...].astype(F32).reshape(OWN, MODEL).astype(BF)
    out_grad = contract_last(cot, wp_v[...]).astype(BF).astype(F32)
    enc_copy.wait()
    embedded = (0.5 * (enc_send[...] + enc_recv[...])).astype(BF)
    query_lin = dot(embedded, wq_v[...])
    lin_q[...] = silu_slope(query_lin)
    queries = silu(query_lin).astype(BF).astype(F32)

    def send(src, dst, ssem, rsem, device):
        pltpu.make_async_remote_copy(
            src_ref=src, dst_ref=dst, send_sem=ssem, recv_sem=rsem,
            device_id=device, device_id_type=pl.DeviceIdType.MESH,
        ).start()

    def whole(ref, ssem, rsem):
        return pltpu.make_async_remote_copy(
            src_ref=ref, dst_ref=ref, send_sem=ssem, recv_sem=rsem,
            device_id=partner, device_id_type=pl.DeviceIdType.MESH,
        )

    def heads_stacked(rows):
        return jnp.concatenate([rows[:, :DH], rows[:, DH:]], axis=0)

    mine = ci * NEAR + spot
    near = pl.ds(ci * NEAR, NEAR)
    far = pl.ds((1 - ci) * NEAR, NEAR)

    def gather_sems(ph, u, n):
        return ag_ssem.at[ph, u, n], ag_rsem.at[ph, u, n]

    def gather_waits(ph, u):
        return (
            whole(ag.at[ph, u, 0 : NEAR - 1], *gather_sems(ph, u, 0)),
            whole(ag.at[ph, u, 0:NEAR], *gather_sems(ph, u, 1)),
        )

    def gather_first(ph, u, block):
        ag[ph, u, mine] = block
        ref = ag.at[ph, u, mine]
        for _, device in peers:
            send(ref, ref, *gather_sems(ph, u, 0), device)

    def gather_last(ph, u):
        gather_waits(ph, u)[0].wait_recv()
        ref = ag.at[ph, u, near]
        send(ref, ref, *gather_sems(ph, u, 1), sibling)

    def gather_end(ph, u):
        gather_waits(ph, u)[1].wait_recv()
        blocks = ag[ph, u].astype(F32)
        for h in range(2):
            rows = blocks[:, h * ROWS : (h + 1) * ROWS, :].reshape(TARGETS, DH)
            rows_v[h] = rows.astype(BF)

    def sum_sems(ph, u, n):
        return rs_ssem.at[ph, u, n], rs_rsem.at[ph, u, n]

    def sum_waits(ph, u):
        return (
            whole(rs1_recv.at[ph, u], *sum_sems(ph, u, 0)),
            whole(rs2_recv.at[ph, u, 0 : NEAR - 1], *sum_sems(ph, u, 1)),
        )

    def sum_first(ph, u):
        rs1_send[ph, u] = sums_v[...].astype(BF)
        send(rs1_send.at[ph, u, far], rs1_recv.at[ph, u], *sum_sems(ph, u, 0), sibling)

    def sum_mid(ph, u):
        sum_waits(ph, u)[0].wait_recv()
        total = rs1_send[ph, u, near].astype(F32) + rs1_recv[ph, u].astype(F32)
        rs2_send[ph, u] = total.astype(BF)
        rs2_recv[ph, u, spot] = rs2_send[ph, u, spot]
        for peer, device in peers:
            send(
                rs2_send.at[ph, u, peer], rs2_recv.at[ph, u, spot], *sum_sems(ph, u, 1), device
            )

    def sum_end(ph, u):
        sum_waits(ph, u)[1].wait_recv()
        return jnp.sum(rs2_recv[ph, u].astype(F32), axis=0)

    for u in range(USERS):
        gather_first(0, u, heads_stacked(queries[u * ROWS : (u + 1) * ROWS]).astype(BF))
    gate_lin = dot(embedded, wg_v[...])
    lin_g[...] = silu_slope(gate_lin)
    gates = silu(gate_lin).astype(BF).astype(F32)
    for u in range(USERS):
        gates_v[u] = heads_stacked(gates[u * ROWS : (u + 1) * ROWS])
        outg_v[u] = heads_stacked(out_grad[u * ROWS : (u + 1) * ROWS])
    gather_last(0, 0)
    gather_last(0, 1)

    def norm_and_gather(u):
        attended = sum_end(0, u)
        grads = outg_v[u]
        rscale = lax.rsqrt(jnp.mean(attended * attended, axis=-1, keepdims=True) + 1e-06)
        normed = attended * rscale
        gateg_v[u] = grads * normed
        ng = grads * gates_v[u]
        grad = rscale * (ng - normed * jnp.mean(ng * normed, axis=-1, keepdims=True))
        gather_first(1, u, grad.astype(BF))

    def query_grad_end(u):
        qgrad_v[u] = sum_end(1, u) * SCALE

    def unstacked(ref):
        return jnp.concatenate(
            [ref[:, h * ROWS : (h + 1) * ROWS, :].reshape(OWN, DH) for h in range(2)], axis=1
        )

    lane = lax.broadcasted_iota(jnp.int32, (1, EVENTS), 1) + base

    def keep(r, h, sums):
        slots = slice(r // ROWS, (r + CUT_ROWS) // ROWS)
        rows = pl.ds(pl.multiple_of(h * ROWS, ROWS), ROWS)
        sums_v[slots, rows, :] = sums.reshape(CUT_ROWS // ROWS, ROWS, DH)

    def forward(u, h):
        cols = pl.ds(pl.multiple_of(h * DH, DH), DH)
        for r in range(0, TARGETS, CUT_ROWS):
            rows = slice(r, r + CUT_ROWS)
            scores = contract_last(rows_v[h, rows, :], k_v[u, :, cols])
            cut = cut_v[u, rows, :]
            visible = lane < jnp.concatenate([cut] * (EVENTS // DH), axis=1)
            y = jnp.where(visible, scores * (0.5 * SCALE), -1e30).astype(BF)
            t = jnp.tanh(y)
            s2 = BF(1) + t
            w = y * s2
            slope_v[u * 2 + h, rows, :] = BF(0.5) * s2 + w * (BF(0.5) - BF(0.5) * t)
            keep(r, h, dot(w, v_v[u, :, cols]))

    def backward(u, h):
        cols = pl.ds(pl.multiple_of(h * DH, DH), DH)
        for r in range(0, TARGETS, CUT_ROWS):
            rows = slice(r, r + CUT_ROWS)
            wgrad = contract_last(rows_v[h, rows, :], v_v[u, :, cols])
            gs = wgrad.astype(BF) * slope_v[u * 2 + h, rows, :]
            keep(r, h, dot(gs, k_v[u, :, cols]))

    @pl.loop(0, 4 * USERS)
    def _(i):
        u = lax.rem(i, 8) // 2
        h = lax.rem(i, 2)

        @pl.when(i < 8)
        def _():
            @pl.when(h == 0)
            def _():
                gather_end(0, u)
                for copy in kv_copies(u):
                    copy.wait()

            forward(u, h)

        @pl.when(i >= 8)
        def _():
            @pl.when(h == 0)
            def _():
                gather_end(1, u)

            backward(u, h)

        @pl.when(h == 1)
        def _():
            sum_first(i // 8, u)

        @pl.when((i == 6) | (i == 7) | (i == 8))
        def _():
            @pl.when(i == 7)
            def _():
                sum_mid(0, 3)

            norm_and_gather(i - 6 + i // 8)

        @pl.when((i == 2) | (i == 4) | (i == 6) | (i == 10) | (i == 12) | (i == 14))
        def _():
            sum_mid(i // 8, lax.rem(i, 8) // 2 - 1)

        @pl.when(i == 7)
        def _():
            gather_last(1, 0)
            norm_and_gather(2)

        @pl.when((i == 8) | (i == 10) | (i == 12))
        def _():
            gather_last(1, i // 2 - 3)

        @pl.when(i == 0)
        def _():
            gather_last(0, 2)
            gather_last(0, 3)

    sum_mid(1, USERS - 1)
    for u in range(USERS):
        query_grad_end(u)

    query_back = (unstacked(qgrad_v) * lin_q[...]).astype(BF)
    gate_back = (unstacked(gateg_v) * lin_g[...]).astype(BF)
    emb_send[...] = (
        contract_last(query_back, wq_v[...]) + contract_last(gate_back, wg_v[...])
    ).astype(BF)
    emb_copy = head_copy(emb_send, emb_recv, 1)
    emb_copy.start()
    emb_copy.wait()
    embed_grad = (0.5 * (emb_send[...].astype(F32) + emb_recv[...].astype(F32))).astype(BF)
    hidden_grad = contract_last(embed_grad, we_v[...])
    hidden_back = jnp.concatenate(
        [(hidden_grad * hid_slope[r * OWN : (r + 1) * OWN, :]).astype(BF) for r in range(EACH)],
        axis=0,
    )
    x_v[...] = hidden_back
    mine = pl.ds(pl.multiple_of(hi * 64, 64), 64)
    other = pl.ds(pl.multiple_of((1 - hi) * 64, 64), 64)
    copies = []
    for j in range(OUT_CHUNKS):
        cols = slice(j * OUT_CHUNK, (j + 1) * OUT_CHUNK)
        part_own[:, cols] = contract_last(x_v[...], wh_v[cols, :])
        part_send[j] = part_own[other, cols].astype(BF)
        copies.append(head_copy(part_send.at[j], part_recv.at[j], 2 + j))
        copies[-1].start()
    for j in range(OUT_CHUNKS):
        cols = slice(j * OUT_CHUNK, (j + 1) * OUT_CHUNK)
        copies[j].wait()
        own = part_own[mine, cols].astype(BF).astype(F32)
        out_ref[:, cols] = (own + part_recv[j].astype(F32)).astype(BF)

    @pl.loop(0, USERS)
    def _(u):
        for ph in range(2):
            for copy in gather_waits(ph, u):
                copy.wait_send()
            for copy in sum_waits(ph, u):
                copy.wait_send()


def body(
    content_rows, w_hidden, w_embed, w_query, w_gate, w_proj,
    history_keys, history_values, cutoffs, out_cotangent,
):
    x = content_rows.transpose(2, 0, 1, 3).reshape(EACH * OWN, WIDTH)
    cut = cutoffs.reshape(USERS, NEAR, 2, ROWS).transpose(0, 2, 1, 3)
    cut = jnp.broadcast_to(cut.reshape(USERS, TARGETS, 1), (USERS, TARGETS, DH))
    dma = pltpu.SemaphoreType.DMA
    v = pltpu.VMEM
    part = pl.pallas_call(
        kernel,
        name="attention_and_encoder",
        out_shape=jax.ShapeDtypeStruct((64, WIDTH), BF),
        in_specs=[pl.BlockSpec(memory_space=pl.ANY)] * 10,
        out_specs=pl.BlockSpec(memory_space=pltpu.VMEM),
        scratch_shapes=[
            v((EACH * OWN, WIDTH), BF), v((WIDTH, HALF), BF), v((HALF, MODEL), BF),
            v((MODEL, LOCAL), BF), v((MODEL, LOCAL), BF), v((LOCAL, MODEL), BF),
            v((USERS, EVENTS, LOCAL), BF), v((USERS, EVENTS, LOCAL), BF),
            v((USERS, TARGETS, DH), jnp.int32), v((USERS, ROWS, MODEL), BF),
            v((2 * USERS, TARGETS, EVENTS), BF), v((EACH * OWN, HALF), F32),
            v((OWN, MODEL), F32), v((OWN, MODEL), F32),
            v((OWN, LOCAL), F32), v((OWN, LOCAL), F32),
            v((USERS, 2 * ROWS, DH), F32), v((USERS, 2 * ROWS, DH), F32),
            v((USERS, 2 * ROWS, DH), F32), v((USERS, 2 * ROWS, DH), F32),
            v((2, USERS, SLOTS, 2 * ROWS, DH), BF), v((2, TARGETS, DH), BF),
            v((SLOTS, 2 * ROWS, DH), F32), v((2, USERS, SLOTS, 2 * ROWS, DH), BF),
            v((2, USERS, NEAR, 2 * ROWS, DH), BF), v((2, USERS, NEAR, 2 * ROWS, DH), BF),
            v((2, USERS, NEAR, 2 * ROWS, DH), BF),
            v((OWN, MODEL), BF), v((OWN, MODEL), BF),
            v((OUT_CHUNKS, 64, OUT_CHUNK), BF), v((OUT_CHUNKS, 64, OUT_CHUNK), BF),
            v((EACH * OWN, WIDTH), F32),
            dma((7 + HID_CHUNKS,)), dma((2, USERS)),
            dma((2, USERS, 2)), dma((2, USERS, 2)), dma((2, USERS, 2)), dma((2, USERS, 2)),
            dma((2 + OUT_CHUNKS,)), dma((2 + OUT_CHUNKS,)),
        ],
        compiler_params=pltpu.CompilerParams(
            collective_id=0, has_side_effects=True, vmem_limit_bytes=62 * 2**20
        ),
    )(
        x, w_hidden, w_embed, w_query, w_gate, w_proj,
        history_keys, history_values, cut, out_cotangent,
    )
    return part.reshape(2, USERS, ROWS, WIDTH).transpose(1, 2, 0, 3)


def solution(mesh):
    split = Mesh(
        mesh.devices.reshape(4, 4, 2, 2, mesh.shape["head"]),
        (*CTX, "head"),
    )
    return jax.shard_map(
        body,
        mesh=split,
        in_specs=(
            P(None, CTX, None, None), P(None, "head"), P("head", None), P(None, "head"),
            P(None, "head"), P("head", None), P(None, CTX, "head"), P(None, CTX, "head"),
            P(), P(None, CTX, None),
        ),
        out_specs=P(None, CTX, "head", None),
        check_vma=False,
    )
```

```python
import jax
import jax.numpy as jnp
from jax import lax
from jax.experimental import pallas as pl
from jax.experimental.pallas import tpu as pltpu
from jax.sharding import Mesh
from jax.sharding import PartitionSpec as P

DH = 128
CTX = ("x", "y", "zh", "c")
BF = jnp.bfloat16
F32 = jnp.float32
LAST = (((1,), (1,)), ((), ()))
USERS, ROWS, EACH, WIDTH = 4, 8, 4, 2048
HALF, MODEL, LOCAL = 2048, 512, 256
TARGETS, EVENTS = 512, 2304
OWN = USERS * ROWS
SLOTS, NEAR = 64, 32
OFFSETS = sorted(
    [(a, b, c) for a in range(4) for b in range(4) for c in range(2) if a or b or c],
    key=lambda t: -(min(t[0], 4 - t[0]) + min(t[1], 4 - t[1]) + 2 * t[2]),
)
CUT_ROWS = 128
HID_CHUNKS = 4
HID_CHUNK = HALF // HID_CHUNKS
OUT_CHUNKS = 4
OUT_CHUNK = WIDTH // OUT_CHUNKS
SCALE = DH**-0.5


def contract_last(left, right):
    return lax.dot_general(left, right, LAST, preferred_element_type=F32)


def dot(left, right):
    return jnp.dot(left, right, preferred_element_type=F32)


def silu(v):
    return v * jax.nn.sigmoid(v)


def silu_slope(v):
    s = jax.nn.sigmoid(v)
    return s * (1.0 + v * (1.0 - s))


def kernel(
    x_hbm, wh_hbm, we_hbm, wq_hbm, wg_hbm, wp_hbm, k_hbm, v_hbm, cut_hbm, cot_hbm,
    out_ref,
    x_in, cut_in, pairs_v, x_v, wh_v, we_v, wq_v, wg_v, wp_v, k_v, v_v, cut_v, cot_v,
    slope_v, hid_slope, enc_send, enc_recv, lin_q, lin_g, gates_v, outg_v, gateg_v, qgrad_v,
    ag, rows_v, sums_v, rs1_send, rs1_recv, rs2_send, rs2_recv,
    emb_send, emb_recv, part_send, part_recv, part_own,
    load_sem, kv_sem, ag_ssem, ag_rsem, rs_ssem, rs_rsem, head_ssem, head_rsem,
):
    xi, yi, zi, ci, hi = (lax.axis_index(a) for a in (*CTX, "head"))
    base = (((xi * 4 + yi) * 2 + zi) * 2 + ci) * EVENTS
    partner = {"head": 1 - hi}
    sibling = {"c": 1 - ci}

    spot = (xi * 4 + yi) * 2 + zi
    peers = []
    for dx, dy, dz in OFFSETS:
        px, py, pz = lax.rem(xi + dx, 4), lax.rem(yi + dy, 4), lax.rem(zi + dz, 2)
        peers.append(((px * 4 + py) * 2 + pz, {"x": px, "y": py, "zh": pz}))

    loads = [pltpu.make_async_copy(x_hbm, x_in, load_sem.at[0])]
    for j in range(HID_CHUNKS):
        cols = pl.ds(j * HID_CHUNK, HID_CHUNK)
        loads.append(
            pltpu.make_async_copy(wh_hbm.at[:, cols], wh_v.at[:, cols], load_sem.at[len(loads)])
        )
    for src, dst in (
        (we_hbm, we_v), (cot_hbm, cot_v), (wp_hbm, wp_v), (wq_hbm, wq_v), (wg_hbm, wg_v),
        (cut_hbm, cut_in),
    ):
        loads.append(pltpu.make_async_copy(src, dst, load_sem.at[len(loads)]))
    for copy in loads:
        copy.start()

    def kv_copies(u):
        return (
            pltpu.make_async_copy(k_hbm.at[u], k_v.at[u], kv_sem.at[0, u]),
            pltpu.make_async_copy(v_hbm.at[u], v_v.at[u], kv_sem.at[1, u]),
        )

    barrier = pltpu.get_barrier_semaphore()
    for device in [partner, sibling] + [device for _, device in peers]:
        pl.semaphore_signal(barrier, inc=1, device_id=device, device_id_type=pl.DeviceIdType.MESH)

    row = lax.broadcasted_iota(jnp.int32, (EACH * OWN, EACH * OWN), 0)
    col = lax.broadcasted_iota(jnp.int32, (EACH * OWN, EACH * OWN), 1)
    target = (row % 64) // 2
    picked = col == target * EACH + (row // 64) * 2 + row % 2
    order = jnp.where(picked, 1.0, 0.0).astype(BF)
    spread = jnp.where(target == col, 1.0, 0.0)[:, :OWN].astype(BF)
    loads[0].wait()
    x_v[...] = dot(order, x_in[...].reshape(EACH * OWN, WIDTH)).astype(BF)
    for j in range(HID_CHUNKS):
        loads[1 + j].wait()
        cols = slice(j * HID_CHUNK, (j + 1) * HID_CHUNK)
        lin = dot(x_v[...], wh_v[:, cols])
        s = jax.nn.sigmoid(lin)
        hidden = lin * s
        hid_slope[:, cols] = s * (1.0 + lin * (1.0 - s))
        if j == 0:
            loads[1 + HID_CHUNKS].wait()
        part = dot(hidden.astype(BF), we_v[cols, :])
        total = part if j == 0 else total + part
    for u in range(USERS):
        for copy in kv_copies(u):
            copy.start()
    for n in range(2 + HID_CHUNKS, 7 + HID_CHUNKS):
        loads[n].wait()
    pairs = total[0:64] + total[64:128]
    for n in range(MODEL // DH):
        cols = slice(n * DH, (n + 1) * DH)
        pairs_v[n] = pairs[:, cols]
        even, odd = (pairs_v[n, pl.ds(k, OWN, stride=2), :] for k in range(2))
        enc_send[:, cols] = even + odd

    pl.semaphore_wait(barrier, 33)

    def head_copy(src, dst, n):
        return pltpu.make_async_remote_copy(
            src_ref=src, dst_ref=dst, send_sem=head_ssem.at[n], recv_sem=head_rsem.at[n],
            device_id=partner, device_id_type=pl.DeviceIdType.MESH,
        )

    enc_copy = head_copy(enc_send, enc_recv, 0)
    enc_copy.start()
    for u in range(USERS):
        limits = jnp.clip(cut_in[u : u + 1, :] - base, 0, EVENTS)
        limits = jnp.broadcast_to(limits, (DH, TARGETS)).T.reshape(NEAR, 2 * ROWS, DH)
        for n in range(2):
            part = limits[:, n * ROWS : (n + 1) * ROWS, :].reshape(TARGETS // 2, DH)
            cut_v[u, n * (TARGETS // 2) : (n + 1) * (TARGETS // 2), :] = part.astype(jnp.int16)
    cot = cot_v[...].astype(F32).reshape(OWN, MODEL).astype(BF)
    out_grad = contract_last(cot, wp_v[...]).astype(BF).astype(F32)
    enc_copy.wait()
    embedded = (0.5 * (enc_send[...] + enc_recv[...])).astype(BF)
    query_lin = dot(embedded, wq_v[...])
    lin_q[...] = silu_slope(query_lin)
    queries = silu(query_lin).astype(BF).astype(F32)

    def send(src, dst, ssem, rsem, device):
        pltpu.make_async_remote_copy(
            src_ref=src, dst_ref=dst, send_sem=ssem, recv_sem=rsem,
            device_id=device, device_id_type=pl.DeviceIdType.MESH,
        ).start()

    def whole(ref, ssem, rsem):
        return pltpu.make_async_remote_copy(
            src_ref=ref, dst_ref=ref, send_sem=ssem, recv_sem=rsem,
            device_id=partner, device_id_type=pl.DeviceIdType.MESH,
        )

    def heads_stacked(rows):
        return jnp.concatenate([rows[:, :DH], rows[:, DH:]], axis=0)

    mine = ci * NEAR + spot
    near = pl.ds(ci * NEAR, NEAR)
    far = pl.ds((1 - ci) * NEAR, NEAR)

    def gather_sems(ph, u, n):
        return ag_ssem.at[ph, u, n], ag_rsem.at[ph, u, n]

    def gather_waits(ph, u):
        return (
            whole(ag.at[ph, u, 0 : NEAR - 1], *gather_sems(ph, u, 0)),
            whole(ag.at[ph, u, 0:NEAR], *gather_sems(ph, u, 1)),
        )

    def gather_first(ph, u, block):
        ag[ph, u, mine] = block
        ref = ag.at[ph, u, mine]
        for _, device in peers:
            send(ref, ref, *gather_sems(ph, u, 0), device)

    def gather_last(ph, u):
        gather_waits(ph, u)[0].wait_recv()
        ref = ag.at[ph, u, near]
        send(ref, ref, *gather_sems(ph, u, 1), sibling)

    def gather_end(ph, u):
        gather_waits(ph, u)[1].wait_recv()
        blocks = ag[ph, u].astype(F32)
        for h in range(2):
            rows = blocks[:, h * ROWS : (h + 1) * ROWS, :].reshape(TARGETS, DH)
            rows_v[h] = rows.astype(BF)

    def sum_sems(ph, u, n):
        return rs_ssem.at[ph, u, n], rs_rsem.at[ph, u, n]

    def sum_waits(ph, u):
        return (
            whole(rs1_recv.at[ph, u], *sum_sems(ph, u, 0)),
            whole(rs2_recv.at[ph, u, 0 : NEAR - 1], *sum_sems(ph, u, 1)),
        )

    def sum_first(ph, u):
        rs1_send[ph, u] = sums_v[...].astype(BF)
        send(rs1_send.at[ph, u, far], rs1_recv.at[ph, u], *sum_sems(ph, u, 0), sibling)

    def sum_mid(ph, u):
        sum_waits(ph, u)[0].wait_recv()
        total = rs1_send[ph, u, near].astype(F32) + rs1_recv[ph, u].astype(F32)
        rs2_send[ph, u] = total.astype(BF)
        rs2_recv[ph, u, spot] = rs2_send[ph, u, spot]
        for peer, device in peers:
            send(
                rs2_send.at[ph, u, peer], rs2_recv.at[ph, u, spot], *sum_sems(ph, u, 1), device
            )

    def sum_end(ph, u):
        sum_waits(ph, u)[1].wait_recv()
        return jnp.sum(rs2_recv[ph, u].astype(F32), axis=0)

    for u in range(USERS):
        gather_first(0, u, heads_stacked(queries[u * ROWS : (u + 1) * ROWS]).astype(BF))
    gate_lin = dot(embedded, wg_v[...])
    lin_g[...] = silu_slope(gate_lin)
    gates = silu(gate_lin).astype(BF).astype(F32)
    for u in range(USERS):
        gates_v[u] = heads_stacked(gates[u * ROWS : (u + 1) * ROWS])
        outg_v[u] = heads_stacked(out_grad[u * ROWS : (u + 1) * ROWS])
    gather_last(0, 0)
    gather_last(0, 1)

    def norm_and_gather(u):
        attended = sum_end(0, u)
        grads = outg_v[u]
        rscale = lax.rsqrt(jnp.mean(attended * attended, axis=-1, keepdims=True) + 1e-06)
        normed = attended * rscale
        gateg_v[u] = grads * normed
        ng = grads * gates_v[u]
        grad = rscale * (ng - normed * jnp.mean(ng * normed, axis=-1, keepdims=True))
        gather_first(1, u, grad.astype(BF))

    def query_grad_end(u):
        qgrad_v[u] = sum_end(1, u) * (0.5 * SCALE)

    def unstacked(ref):
        return jnp.concatenate(
            [ref[:, h * ROWS : (h + 1) * ROWS, :].reshape(OWN, DH) for h in range(2)], axis=1
        )

    lane = lax.broadcasted_iota(jnp.int32, (2 * ROWS, EVENTS), 1).astype(jnp.int16)
    lane = jnp.concatenate([lane] * (CUT_ROWS // (2 * ROWS)), axis=0)

    def keep(r, h, sums):
        slots = slice(r // ROWS, (r + CUT_ROWS) // ROWS)
        rows = pl.ds(pl.multiple_of(h * ROWS, ROWS), ROWS)
        sums_v[slots, rows, :] = sums.reshape(CUT_ROWS // ROWS, ROWS, DH)

    def forward(u, h):
        cols = pl.ds(pl.multiple_of(h * DH, DH), DH)
        for r in range(0, TARGETS, CUT_ROWS):
            rows = slice(r, r + CUT_ROWS)
            scores = contract_last(rows_v[h, rows, :], k_v[u, :, cols])
            cut = cut_v[u, rows, :]
            visible = lane < jnp.concatenate([cut] * (EVENTS // DH), axis=1)
            y = (scores * (0.5 * SCALE)).astype(BF)
            t = jnp.where(visible, jnp.tanh(y), BF(-1))
            s2 = BF(1) + t
            w = y * s2
            slope_v[u * 2 + h, rows, :] = s2 + w * (BF(1) - t)
            keep(r, h, dot(w, v_v[u, :, cols]))

    def backward(u, h):
        cols = pl.ds(pl.multiple_of(h * DH, DH), DH)
        for r in range(0, TARGETS, CUT_ROWS):
            rows = slice(r, r + CUT_ROWS)
            wgrad = contract_last(rows_v[h, rows, :], v_v[u, :, cols])
            gs = wgrad.astype(BF) * slope_v[u * 2 + h, rows, :]
            keep(r, h, dot(gs, k_v[u, :, cols]))

    @pl.loop(0, 4 * USERS)
    def _(i):
        u = lax.rem(i, 8) // 2
        h = lax.rem(i, 2)

        @pl.when(i < 8)
        def _():
            @pl.when(h == 0)
            def _():
                gather_end(0, u)
                for copy in kv_copies(u):
                    copy.wait()

            forward(u, h)

        @pl.when(i >= 8)
        def _():
            @pl.when(h == 0)
            def _():
                gather_end(1, u)

            backward(u, h)

        @pl.when(h == 1)
        def _():
            sum_first(i // 8, u)

        @pl.when((i == 6) | (i == 7) | (i == 8))
        def _():
            @pl.when(i == 7)
            def _():
                sum_mid(0, 3)

            norm_and_gather(i - 6 + i // 8)

        @pl.when((i == 2) | (i == 4) | (i == 6) | (i == 10) | (i == 12) | (i == 14))
        def _():
            sum_mid(i // 8, lax.rem(i, 8) // 2 - 1)

        @pl.when(i == 7)
        def _():
            gather_last(1, 0)
            norm_and_gather(2)

        @pl.when((i == 8) | (i == 10) | (i == 12))
        def _():
            gather_last(1, i // 2 - 3)

        @pl.when(i == 0)
        def _():
            gather_last(0, 2)
            gather_last(0, 3)

    sum_mid(1, USERS - 1)
    for u in range(USERS):
        query_grad_end(u)

    query_back = (unstacked(qgrad_v) * lin_q[...]).astype(BF)
    gate_back = (unstacked(gateg_v) * lin_g[...]).astype(BF)
    emb_send[...] = (
        contract_last(query_back, wq_v[...]) + contract_last(gate_back, wg_v[...])
    ).astype(BF)
    emb_copy = head_copy(emb_send, emb_recv, 1)
    emb_copy.start()
    emb_copy.wait()
    embed_grad = (0.5 * (emb_send[...].astype(F32) + emb_recv[...].astype(F32))).astype(BF)
    hidden_grad = contract_last(dot(spread, embed_grad).astype(BF), we_v[...])
    x_v[...] = (hidden_grad * hid_slope[...]).astype(BF)
    mine = pl.ds(pl.multiple_of(hi * 64, 64), 64)
    other = pl.ds(pl.multiple_of((1 - hi) * 64, 64), 64)
    copies = []
    for j in range(OUT_CHUNKS):
        cols = slice(j * OUT_CHUNK, (j + 1) * OUT_CHUNK)
        part_own[:, cols] = contract_last(x_v[...], wh_v[cols, :])
        part_send[j] = part_own[other, cols].astype(BF)
        copies.append(head_copy(part_send.at[j], part_recv.at[j], 2 + j))
        copies[-1].start()
    for j in range(OUT_CHUNKS):
        cols = slice(j * OUT_CHUNK, (j + 1) * OUT_CHUNK)
        copies[j].wait()
        own = part_own[mine, cols].astype(BF).astype(F32)
        out_ref[:, cols] = (own + part_recv[j].astype(F32)).astype(BF)

    @pl.loop(0, USERS)
    def _(u):
        for ph in range(2):
            for copy in gather_waits(ph, u):
                copy.wait_send()
            for copy in sum_waits(ph, u):
                copy.wait_send()


def body(
    content_rows, w_hidden, w_embed, w_query, w_gate, w_proj,
    history_keys, history_values, cutoffs, out_cotangent,
):
    dma = pltpu.SemaphoreType.DMA
    v = pltpu.VMEM
    part = pl.pallas_call(
        kernel,
        name="attention_and_encoder",
        out_shape=jax.ShapeDtypeStruct((64, WIDTH), BF),
        in_specs=[pl.BlockSpec(memory_space=pl.ANY)] * 10,
        out_specs=pl.BlockSpec(memory_space=pltpu.VMEM),
        scratch_shapes=[
            v((USERS, ROWS, EACH, WIDTH), BF), v((USERS, TARGETS), jnp.int32), v((MODEL // DH, 64, DH), F32),
            v((EACH * OWN, WIDTH), BF), v((WIDTH, HALF), BF), v((HALF, MODEL), BF),
            v((MODEL, LOCAL), BF), v((MODEL, LOCAL), BF), v((LOCAL, MODEL), BF),
            v((USERS, EVENTS, LOCAL), BF), v((USERS, EVENTS, LOCAL), BF),
            v((USERS, TARGETS, DH), jnp.int16), v((USERS, ROWS, MODEL), BF),
            v((2 * USERS, TARGETS, EVENTS), BF), v((EACH * OWN, HALF), F32),
            v((OWN, MODEL), F32), v((OWN, MODEL), F32),
            v((OWN, LOCAL), F32), v((OWN, LOCAL), F32),
            v((USERS, 2 * ROWS, DH), F32), v((USERS, 2 * ROWS, DH), F32),
            v((USERS, 2 * ROWS, DH), F32), v((USERS, 2 * ROWS, DH), F32),
            v((2, USERS, SLOTS, 2 * ROWS, DH), BF), v((2, TARGETS, DH), BF),
            v((SLOTS, 2 * ROWS, DH), F32), v((2, USERS, SLOTS, 2 * ROWS, DH), BF),
            v((2, USERS, NEAR, 2 * ROWS, DH), BF), v((2, USERS, NEAR, 2 * ROWS, DH), BF),
            v((2, USERS, NEAR, 2 * ROWS, DH), BF),
            v((OWN, MODEL), BF), v((OWN, MODEL), BF),
            v((OUT_CHUNKS, 64, OUT_CHUNK), BF), v((OUT_CHUNKS, 64, OUT_CHUNK), BF),
            v((EACH * OWN, WIDTH), F32),
            dma((7 + HID_CHUNKS,)), dma((2, USERS)),
            dma((2, USERS, 2)), dma((2, USERS, 2)), dma((2, USERS, 2)), dma((2, USERS, 2)),
            dma((2 + OUT_CHUNKS,)), dma((2 + OUT_CHUNKS,)),
        ],
        compiler_params=pltpu.CompilerParams(
            collective_id=0, has_side_effects=True, vmem_limit_bytes=62 * 2**20
        ),
    )(
        content_rows, w_hidden, w_embed, w_query, w_gate, w_proj,
        history_keys, history_values, cutoffs, out_cotangent,
    )
    return part.reshape(USERS, ROWS, 2, WIDTH)


def solution(mesh):
    split = Mesh(
        mesh.devices.reshape(4, 4, 2, 2, mesh.shape["head"]),
        (*CTX, "head"),
    )
    return jax.shard_map(
        body,
        mesh=split,
        in_specs=(
            P(None, CTX, None, None), P(None, "head"), P("head", None), P(None, "head"),
            P(None, "head"), P("head", None), P(None, CTX, "head"), P(None, CTX, "head"),
            P(), P(None, CTX, None),
        ),
        out_specs=P(None, CTX, "head", None),
        check_vma=False,
    )
```

```python
import jax
import jax.numpy as jnp
from jax import lax
from jax.experimental import pallas as pl
from jax.experimental.pallas import tpu as pltpu
from jax.sharding import Mesh
from jax.sharding import PartitionSpec as P

DH = 128
CTX = ("x", "y", "zh", "c")
BF = jnp.bfloat16
F32 = jnp.float32
LAST = (((1,), (1,)), ((), ()))
USERS, ROWS, EACH, WIDTH = 4, 8, 4, 2048
HALF, MODEL, LOCAL = 2048, 512, 256
TARGETS, EVENTS = 512, 2304
OWN = USERS * ROWS
GROUP = 2 * ROWS
SLOTS, NEAR = 64, 32
OFFSETS = sorted(
    [(a, b, c) for a in range(4) for b in range(4) for c in range(2) if a or b or c],
    key=lambda t: -(min(t[0], 4 - t[0]) + min(t[1], 4 - t[1]) + 2 * t[2]),
)
HID_CHUNKS = 4
HID_CHUNK = HALF // HID_CHUNKS
OUT_CHUNKS = 4
OUT_CHUNK = WIDTH // OUT_CHUNKS
SCALE = DH**-0.5


def contract_last(left, right):
    return lax.dot_general(left, right, LAST, preferred_element_type=F32)


def contract_first(left, right):
    return lax.dot_general(left, right, (((0,), (0,)), ((), ())), preferred_element_type=F32)


def dot(left, right):
    return jnp.dot(left, right, preferred_element_type=F32)


def silu(v):
    return v * jax.nn.sigmoid(v)


def silu_slope(v):
    s = jax.nn.sigmoid(v)
    return s * (1.0 + v * (1.0 - s))


def kernel(
    x_hbm, wh_hbm, we_hbm, wq_hbm, wg_hbm, wp_hbm, k_hbm, v_hbm, cut_hbm, cot_hbm,
    out_ref,
    x_in, cut_in, pairs_v, x_v, wh_v, we_v, wq_v, wg_v, wp_v, k_v, v_v, cut_v, cot_v,
    slope_v, hid_slope, enc_send, enc_recv, lin_q, lin_g, gates_v, outg_v, gateg_v, qgrad_v,
    ag, rows_v, sums_v, rs1_send, rs1_recv, rs2_send, rs2_recv,
    emb_send, emb_recv, part_send, part_recv, part_own,
    load_sem, kv_sem, ag_ssem, ag_rsem, rs_ssem, rs_rsem, head_ssem, head_rsem,
):
    xi, yi, zi, ci, hi = (lax.axis_index(a) for a in (*CTX, "head"))
    base = (((xi * 4 + yi) * 2 + zi) * 2 + ci) * EVENTS
    partner = {"head": 1 - hi}
    sibling = {"c": 1 - ci}

    spot = (xi * 4 + yi) * 2 + zi
    peers = []
    for dx, dy, dz in OFFSETS:
        px, py, pz = lax.rem(xi + dx, 4), lax.rem(yi + dy, 4), lax.rem(zi + dz, 2)
        peers.append(((px * 4 + py) * 2 + pz, {"x": px, "y": py, "zh": pz}))

    barrier = pltpu.get_barrier_semaphore()
    for device in [partner, sibling] + [device for _, device in peers]:
        pl.semaphore_signal(barrier, inc=1, device_id=device, device_id_type=pl.DeviceIdType.MESH)

    loads = [pltpu.make_async_copy(x_hbm, x_in, load_sem.at[0])]
    for j in range(HID_CHUNKS):
        cols = pl.ds(j * HID_CHUNK, HID_CHUNK)
        loads.append(
            pltpu.make_async_copy(wh_hbm.at[:, cols], wh_v.at[:, cols], load_sem.at[len(loads)])
        )
    for src, dst in (
        (we_hbm, we_v), (cot_hbm, cot_v), (wp_hbm, wp_v), (wq_hbm, wq_v), (wg_hbm, wg_v),
        (cut_hbm, cut_in),
    ):
        loads.append(pltpu.make_async_copy(src, dst, load_sem.at[len(loads)]))
    for copy in loads:
        copy.start()

    def kv_copies(u):
        return (
            pltpu.make_async_copy(k_hbm.at[u], k_v.at[u], kv_sem.at[0, u]),
            pltpu.make_async_copy(v_hbm.at[u], v_v.at[u], kv_sem.at[1, u]),
        )

    row = lax.broadcasted_iota(jnp.int32, (EACH * OWN, EACH * OWN), 0)
    col = lax.broadcasted_iota(jnp.int32, (EACH * OWN, EACH * OWN), 1)
    target = (row // 64) * GROUP + (row % 32) // 2
    picked = col == target * EACH + ((row % 64) // 32) * 2 + row % 2
    order = jnp.where(picked, 1.0, 0.0).astype(BF)
    spread = jnp.where(target == col, 1.0, 0.0)[:, :OWN].astype(BF)
    loads[0].wait()
    x_v[...] = dot(order, x_in[...].reshape(EACH * OWN, WIDTH)).astype(BF)
    for j in range(HID_CHUNKS):
        loads[1 + j].wait()
        cols = slice(j * HID_CHUNK, (j + 1) * HID_CHUNK)
        lin = dot(x_v[...], wh_v[:, cols])
        s = jax.nn.sigmoid(lin)
        hidden = lin * s
        hid_slope[:, cols] = s * (1.0 + lin * (1.0 - s))
        if j == 0:
            loads[1 + HID_CHUNKS].wait()
        part = dot(hidden.astype(BF), we_v[cols, :])
        total = part if j == 0 else total + part
    for u in range(USERS):
        for copy in kv_copies(u):
            copy.start()
    for n in range(2 + HID_CHUNKS, 7 + HID_CHUNKS):
        loads[n].wait()
    pairs = jnp.concatenate([total[0:32] + total[32:64], total[64:96] + total[96:128]], axis=0)
    for n in range(MODEL // DH):
        cols = slice(n * DH, (n + 1) * DH)
        pairs_v[n] = pairs[:, cols]
        even, odd = (pairs_v[n, pl.ds(k, OWN, stride=2), :] for k in range(2))
        enc_send[:, cols] = even + odd

    pl.semaphore_wait(barrier, 33)

    def head_copy(src, dst, n):
        return pltpu.make_async_remote_copy(
            src_ref=src, dst_ref=dst, send_sem=head_ssem.at[n], recv_sem=head_rsem.at[n],
            device_id=partner, device_id_type=pl.DeviceIdType.MESH,
        )

    enc_copy = head_copy(enc_send, enc_recv, 0)
    enc_copy.start()
    for u in range(USERS):
        limits = jnp.clip(cut_in[u : u + 1, :] - base, 0, EVENTS)
        limits = jnp.broadcast_to(limits, (DH, TARGETS)).T.reshape(NEAR, 2 * ROWS, DH)
        halves = [limits[:, n * ROWS : (n + 1) * ROWS, :].reshape(TARGETS // 2, DH) for n in range(2)]
        cut_v[u] = jnp.concatenate(halves, axis=0).T[: 2 * ROWS, :].astype(jnp.int16)
    cot = cot_v[...].astype(F32).reshape(OWN, MODEL).astype(BF)
    out_grad = contract_last(cot, wp_v[...]).astype(BF).astype(F32)
    enc_copy.wait()
    embedded = (0.5 * (enc_send[...] + enc_recv[...])).astype(BF)
    query_lin = dot(embedded, wq_v[...])
    lin_q[...] = silu_slope(query_lin)
    queries = silu(query_lin).astype(BF).astype(F32)

    def send(src, dst, ssem, rsem, device):
        pltpu.make_async_remote_copy(
            src_ref=src, dst_ref=dst, send_sem=ssem, recv_sem=rsem,
            device_id=device, device_id_type=pl.DeviceIdType.MESH,
        ).start()

    def whole(ref, ssem, rsem):
        return pltpu.make_async_remote_copy(
            src_ref=ref, dst_ref=ref, send_sem=ssem, recv_sem=rsem,
            device_id=partner, device_id_type=pl.DeviceIdType.MESH,
        )

    def heads_stacked(rows):
        return jnp.concatenate([rows[:, :DH], rows[:, DH:]], axis=0)

    mine = ci * NEAR + spot
    near = pl.ds(ci * NEAR, NEAR)
    far = pl.ds((1 - ci) * NEAR, NEAR)

    def gather_sems(ph, u, n):
        return ag_ssem.at[ph, u, n], ag_rsem.at[ph, u, n]

    def gather_waits(ph, u):
        return (
            whole(ag.at[ph, u, 0 : NEAR - 1], *gather_sems(ph, u, 0)),
            whole(ag.at[ph, u, 0:NEAR], *gather_sems(ph, u, 1)),
        )

    def gather_first(ph, u, block):
        ag[ph, u, mine] = block
        ref = ag.at[ph, u, mine]
        for _, device in peers:
            send(ref, ref, *gather_sems(ph, u, 0), device)

    def gather_last(ph, u):
        gather_waits(ph, u)[0].wait_recv()
        ref = ag.at[ph, u, near]
        send(ref, ref, *gather_sems(ph, u, 1), sibling)

    def gather_end(ph, u):
        gather_waits(ph, u)[1].wait_recv()
        blocks = ag[ph, u].astype(F32)
        for h in range(2):
            rows = blocks[:, h * ROWS : (h + 1) * ROWS, :].reshape(TARGETS, DH)
            rows_v[h] = rows.astype(BF)

    def sum_sems(ph, u, n):
        return rs_ssem.at[ph, u, n], rs_rsem.at[ph, u, n]

    def sum_waits(ph, u):
        return (
            whole(rs1_recv.at[ph, u], *sum_sems(ph, u, 0)),
            whole(rs2_recv.at[ph, u, 0 : NEAR - 1], *sum_sems(ph, u, 1)),
        )

    def sum_first(ph, u):
        rs1_send[ph, u] = sums_v[...].astype(BF)
        send(rs1_send.at[ph, u, far], rs1_recv.at[ph, u], *sum_sems(ph, u, 0), sibling)

    def sum_mid(ph, u):
        sum_waits(ph, u)[0].wait_recv()
        total = rs1_send[ph, u, near].astype(F32) + rs1_recv[ph, u].astype(F32)
        rs2_send[ph, u] = total.astype(BF)
        rs2_recv[ph, u, spot] = rs2_send[ph, u, spot]
        for peer, device in peers:
            send(
                rs2_send.at[ph, u, peer], rs2_recv.at[ph, u, spot], *sum_sems(ph, u, 1), device
            )

    def sum_end(ph, u):
        sum_waits(ph, u)[1].wait_recv()
        return jnp.sum(rs2_recv[ph, u].astype(F32), axis=0)

    for u in range(USERS):
        gather_first(0, u, heads_stacked(queries[u * ROWS : (u + 1) * ROWS]).astype(BF))
    gate_lin = dot(embedded, wg_v[...])
    lin_g[...] = silu_slope(gate_lin)
    gates = silu(gate_lin).astype(BF).astype(F32)
    for u in range(USERS):
        gates_v[u] = heads_stacked(gates[u * ROWS : (u + 1) * ROWS])
        outg_v[u] = heads_stacked(out_grad[u * ROWS : (u + 1) * ROWS])
    gather_last(0, 0)
    gather_last(0, 1)

    def norm_and_gather(u):
        attended = sum_end(0, u)
        grads = outg_v[u]
        rscale = lax.rsqrt(jnp.mean(attended * attended, axis=-1, keepdims=True) + 1e-06)
        normed = attended * rscale
        gateg_v[u] = grads * normed
        ng = grads * gates_v[u]
        grad = rscale * (ng - normed * jnp.mean(ng * normed, axis=-1, keepdims=True))
        gather_first(1, u, grad.astype(BF))

    def query_grad_end(u):
        qgrad_v[u] = sum_end(1, u) * (0.5 * SCALE)

    def unstacked(ref, g):
        blocks = [ref[2 * g : 2 * g + 2, h * ROWS : (h + 1) * ROWS, :] for h in range(2)]
        return jnp.concatenate([block.reshape(GROUP, DH) for block in blocks], axis=1)

    def keep(h, sums):
        rows = pl.ds(pl.multiple_of(h * ROWS, ROWS), ROWS)
        sums_v[:, rows, :] = sums.T.reshape(SLOTS, ROWS, DH)

    def forward(u, h):
        cols = pl.ds(pl.multiple_of(h * DH, DH), DH)
        scores = contract_last(k_v[u, :, cols], rows_v[h])
        place = lax.broadcasted_iota(jnp.int32, (EVENTS, TARGETS), 0).astype(jnp.int16)
        visible = place < jnp.concatenate([cut_v[u]] * (EVENTS // (2 * ROWS)), axis=0)
        y = (scores * (0.5 * SCALE)).astype(BF)
        t = jnp.where(visible, jnp.tanh(y), BF(-1))
        s2 = BF(1) + t
        w = y * s2
        slope_v[u * 2 + h] = s2 + w * (BF(1) - t)
        keep(h, contract_first(v_v[u, :, cols], w))

    def backward(u, h):
        cols = pl.ds(pl.multiple_of(h * DH, DH), DH)
        wgrad = contract_last(v_v[u, :, cols], rows_v[h])
        gs = wgrad.astype(BF) * slope_v[u * 2 + h]
        keep(h, contract_first(k_v[u, :, cols], gs))

    @pl.loop(0, 4 * USERS)
    def _(i):
        u = lax.rem(i, 8) // 2
        h = lax.rem(i, 2)

        @pl.when(i < 8)
        def _():
            @pl.when(h == 0)
            def _():
                gather_end(0, u)
                for copy in kv_copies(u):
                    copy.wait()

            forward(u, h)

        @pl.when(i >= 8)
        def _():
            @pl.when(h == 0)
            def _():
                gather_end(1, u)

            backward(u, h)

        @pl.when(h == 1)
        def _():
            sum_first(i // 8, u)

        @pl.when((i == 6) | (i == 7) | (i == 8))
        def _():
            @pl.when(i == 7)
            def _():
                sum_mid(0, 3)

            norm_and_gather(i - 6 + i // 8)

        @pl.when((i == 2) | (i == 4) | (i == 6) | (i == 10) | (i == 12) | (i == 14))
        def _():
            sum_mid(i // 8, lax.rem(i, 8) // 2 - 1)

        @pl.when(i == 7)
        def _():
            gather_last(1, 0)
            norm_and_gather(2)

        @pl.when((i == 8) | (i == 10) | (i == 12))
        def _():
            gather_last(1, i // 2 - 3)

        @pl.when(i == 0)
        def _():
            gather_last(0, 2)
            gather_last(0, 3)

    sum_mid(1, USERS - 1)

    emb_copies, part_copies = [], []

    def embed_part(g):
        rows = slice(g * GROUP, (g + 1) * GROUP)
        for u in (2 * g, 2 * g + 1):
            query_grad_end(u)
        query_back = (unstacked(qgrad_v, g) * lin_q[rows, :]).astype(BF)
        gate_back = (unstacked(gateg_v, g) * lin_g[rows, :]).astype(BF)
        emb_send[g] = (
            contract_last(query_back, wq_v[...]) + contract_last(gate_back, wg_v[...])
        ).astype(BF)
        emb_copies.append(head_copy(emb_send.at[g], emb_recv.at[g], 1 + g))
        emb_copies[g].start()

    def content_part(g):
        emb_copies[g].wait()
        embed_grad = (0.5 * (emb_send[g].astype(F32) + emb_recv[g].astype(F32))).astype(BF)
        rows = slice(g * 64, (g + 1) * 64)
        spread_here = spread[rows, g * GROUP : (g + 1) * GROUP]
        hidden_grad = contract_last(dot(spread_here, embed_grad).astype(BF), we_v[...])
        x_v[rows, :] = (hidden_grad * hid_slope[rows, :]).astype(BF)
        other = pl.ds(pl.multiple_of((1 - hi) * 32, 32), 32)
        for j in range(OUT_CHUNKS):
            cols = slice(j * OUT_CHUNK, (j + 1) * OUT_CHUNK)
            part_own[g, :, cols] = contract_last(x_v[rows, :], wh_v[cols, :])
            part_send[g, j] = part_own[g, other, cols].astype(BF)
            n = g * OUT_CHUNKS + j
            part_copies.append(head_copy(part_send.at[g, j], part_recv.at[g, j], 3 + n))
            part_copies[n].start()

    def content_end(g):
        mine = pl.ds(pl.multiple_of(hi * 32, 32), 32)
        for j in range(OUT_CHUNKS):
            cols = slice(j * OUT_CHUNK, (j + 1) * OUT_CHUNK)
            part_copies[g * OUT_CHUNKS + j].wait()
            own = part_own[g, mine, cols].astype(BF).astype(F32)
            total = (own + part_recv[g, j].astype(F32)).astype(BF)
            out_ref[2 * g : 2 * g + 2, :, :, cols] = total.reshape(2, ROWS, 2, OUT_CHUNK)

    embed_part(0)
    content_part(0)
    embed_part(1)
    content_end(0)
    content_part(1)
    content_end(1)

    @pl.loop(0, USERS)
    def _(u):
        for ph in range(2):
            for copy in gather_waits(ph, u):
                copy.wait_send()
            for copy in sum_waits(ph, u):
                copy.wait_send()


def body(
    content_rows, w_hidden, w_embed, w_query, w_gate, w_proj,
    history_keys, history_values, cutoffs, out_cotangent,
):
    dma = pltpu.SemaphoreType.DMA
    v = pltpu.VMEM
    part = pl.pallas_call(
        kernel,
        name="attention_and_encoder",
        out_shape=jax.ShapeDtypeStruct((USERS, ROWS, 2, WIDTH), BF),
        in_specs=[pl.BlockSpec(memory_space=pl.ANY)] * 10,
        out_specs=pl.BlockSpec(memory_space=pltpu.VMEM),
        scratch_shapes=[
            v((USERS, ROWS, EACH, WIDTH), BF), v((USERS, TARGETS), jnp.int32), v((MODEL // DH, 64, DH), F32),
            v((EACH * OWN, WIDTH), BF), v((WIDTH, HALF), BF), v((HALF, MODEL), BF),
            v((MODEL, LOCAL), BF), v((MODEL, LOCAL), BF), v((LOCAL, MODEL), BF),
            v((USERS, EVENTS, LOCAL), BF), v((USERS, EVENTS, LOCAL), BF),
            v((USERS, 2 * ROWS, TARGETS), jnp.int16), v((USERS, ROWS, MODEL), BF),
            v((2 * USERS, EVENTS, TARGETS), BF), v((EACH * OWN, HALF), F32),
            v((OWN, MODEL), F32), v((OWN, MODEL), F32),
            v((OWN, LOCAL), F32), v((OWN, LOCAL), F32),
            v((USERS, 2 * ROWS, DH), F32), v((USERS, 2 * ROWS, DH), F32),
            v((USERS, 2 * ROWS, DH), F32), v((USERS, 2 * ROWS, DH), F32),
            v((2, USERS, SLOTS, 2 * ROWS, DH), BF), v((2, TARGETS, DH), BF),
            v((SLOTS, 2 * ROWS, DH), F32), v((2, USERS, SLOTS, 2 * ROWS, DH), BF),
            v((2, USERS, NEAR, 2 * ROWS, DH), BF), v((2, USERS, NEAR, 2 * ROWS, DH), BF),
            v((2, USERS, NEAR, 2 * ROWS, DH), BF),
            v((2, GROUP, MODEL), BF), v((2, GROUP, MODEL), BF),
            v((2, OUT_CHUNKS, 32, OUT_CHUNK), BF), v((2, OUT_CHUNKS, 32, OUT_CHUNK), BF),
            v((2, 64, WIDTH), F32),
            dma((7 + HID_CHUNKS,)), dma((2, USERS)),
            dma((2, USERS, 2)), dma((2, USERS, 2)), dma((2, USERS, 2)), dma((2, USERS, 2)),
            dma((3 + 2 * OUT_CHUNKS,)), dma((3 + 2 * OUT_CHUNKS,)),
        ],
        compiler_params=pltpu.CompilerParams(
            collective_id=0, has_side_effects=True, vmem_limit_bytes=62 * 2**20
        ),
    )(
        content_rows, w_hidden, w_embed, w_query, w_gate, w_proj,
        history_keys, history_values, cutoffs, out_cotangent,
    )
    return part


def solution(mesh):
    split = Mesh(
        mesh.devices.reshape(4, 4, 2, 2, mesh.shape["head"]),
        (*CTX, "head"),
    )
    return jax.shard_map(
        body,
        mesh=split,
        in_specs=(
            P(None, CTX, None, None), P(None, "head"), P("head", None), P(None, "head"),
            P(None, "head"), P("head", None), P(None, CTX, "head"), P(None, CTX, "head"),
            P(), P(None, CTX, None),
        ),
        out_specs=P(None, CTX, "head", None),
        check_vma=False,
    )
```

```python
import jax
import jax.numpy as jnp
from jax import lax
from jax.experimental import pallas as pl
from jax.experimental.pallas import tpu as pltpu
from jax.sharding import Mesh
from jax.sharding import PartitionSpec as P

DH = 128
CTX = ("x", "y", "zh", "c")
BF = jnp.bfloat16
F32 = jnp.float32
LAST = (((1,), (1,)), ((), ()))
USERS, ROWS, EACH, WIDTH = 4, 8, 4, 2048
HALF, MODEL, LOCAL = 2048, 512, 256
TARGETS, EVENTS = 512, 2304
OWN = USERS * ROWS
GROUP = 2 * ROWS
SLOTS, NEAR = 64, 32
OFFSETS = sorted(
    [(a, b, c) for a in range(4) for b in range(4) for c in range(2) if a or b or c],
    key=lambda t: -(min(t[0], 4 - t[0]) + min(t[1], 4 - t[1]) + 2 * t[2]),
)
HID_CHUNKS = 4
HID_CHUNK = HALF // HID_CHUNKS
OUT_CHUNKS = 4
OUT_CHUNK = WIDTH // OUT_CHUNKS
SCALE = DH**-0.5


def contract_last(left, right):
    return lax.dot_general(left, right, LAST, preferred_element_type=F32)


def contract_first(left, right):
    return lax.dot_general(left, right, (((0,), (0,)), ((), ())), preferred_element_type=F32)


def dot(left, right):
    return jnp.dot(left, right, preferred_element_type=F32)


def silu(v):
    return v * jax.nn.sigmoid(v)


def silu_slope(v):
    s = jax.nn.sigmoid(v)
    return s * (1.0 + v * (1.0 - s))


def kernel(
    x_hbm, wh_hbm, we_hbm, wq_hbm, wg_hbm, wp_hbm, k_hbm, v_hbm, cut_hbm, cot_hbm,
    out_ref,
    x_in, cut_in, pairs_v, x_v, wh_v, we_v, wq_v, wg_v, wp_v, k_v, v_v, cut_v, cot_v,
    slope_v, hid_slope, enc_send, enc_recv, lin_q, lin_g, gates_v, outg_v, gateg_v, qgrad_v,
    ag, rows_v, sums_v, rs1_send, rs1_recv, rs2_send, rs2_recv,
    emb_send, emb_recv, part_send, part_recv, part_own,
    load_sem, kv_sem, ag_ssem, ag_rsem, rs_ssem, rs_rsem, head_ssem, head_rsem,
):
    xi, yi, zi, ci, hi = (lax.axis_index(a) for a in (*CTX, "head"))
    base = (((xi * 4 + yi) * 2 + zi) * 2 + ci) * EVENTS
    partner = {"head": 1 - hi}
    sibling = {"c": 1 - ci}

    spot = (xi * 4 + yi) * 2 + zi
    peers = []
    for dx, dy, dz in OFFSETS:
        px, py, pz = lax.rem(xi + dx, 4), lax.rem(yi + dy, 4), lax.rem(zi + dz, 2)
        peers.append(((px * 4 + py) * 2 + pz, {"x": px, "y": py, "zh": pz}))

    barrier = pltpu.get_barrier_semaphore()
    for device in [partner, sibling] + [device for _, device in peers]:
        pl.semaphore_signal(barrier, inc=1, device_id=device, device_id_type=pl.DeviceIdType.MESH)

    loads = [pltpu.make_async_copy(x_hbm, x_in, load_sem.at[0])]
    for j in range(HID_CHUNKS):
        cols = pl.ds(j * HID_CHUNK, HID_CHUNK)
        loads.append(
            pltpu.make_async_copy(wh_hbm.at[:, cols], wh_v.at[:, cols], load_sem.at[len(loads)])
        )
    for src, dst in (
        (we_hbm, we_v), (cot_hbm, cot_v), (wp_hbm, wp_v), (wq_hbm, wq_v), (wg_hbm, wg_v),
        (cut_hbm, cut_in),
    ):
        loads.append(pltpu.make_async_copy(src, dst, load_sem.at[len(loads)]))
    for copy in loads:
        copy.start()

    def kv_copies(u):
        return (
            pltpu.make_async_copy(k_hbm.at[u], k_v.at[u], kv_sem.at[0, u]),
            pltpu.make_async_copy(v_hbm.at[u], v_v.at[u], kv_sem.at[1, u]),
        )

    row = lax.broadcasted_iota(jnp.int32, (EACH * OWN, EACH * OWN), 0)
    col = lax.broadcasted_iota(jnp.int32, (EACH * OWN, EACH * OWN), 1)
    target = (row // 64) * GROUP + (row % 32) // 2
    picked = col == target * EACH + ((row % 64) // 32) * 2 + row % 2
    order = jnp.where(picked, 1.0, 0.0).astype(BF)
    spread = jnp.where(target == col, 1.0, 0.0)[:, :OWN].astype(BF)
    loads[0].wait()
    x_v[...] = dot(order, x_in[...].reshape(EACH * OWN, WIDTH)).astype(BF)
    for j in range(HID_CHUNKS):
        loads[1 + j].wait()
        cols = slice(j * HID_CHUNK, (j + 1) * HID_CHUNK)
        lin = dot(x_v[...], wh_v[:, cols])
        s = jax.nn.sigmoid(lin)
        hidden = lin * s
        hid_slope[:, cols] = s * (1.0 + lin * (1.0 - s))
        if j == 0:
            loads[1 + HID_CHUNKS].wait()
        part = dot(hidden.astype(BF), we_v[cols, :])
        total = part if j == 0 else total + part
    for u in range(USERS):
        for copy in kv_copies(u):
            copy.start()
    for n in range(2 + HID_CHUNKS, 7 + HID_CHUNKS):
        loads[n].wait()
    pairs = jnp.concatenate([total[0:32] + total[32:64], total[64:96] + total[96:128]], axis=0)
    for n in range(MODEL // DH):
        cols = slice(n * DH, (n + 1) * DH)
        pairs_v[n] = pairs[:, cols]
        even, odd = (pairs_v[n, pl.ds(k, OWN, stride=2), :] for k in range(2))
        enc_send[:, cols] = even + odd

    pl.semaphore_wait(barrier, 33)

    def head_copy(src, dst, n):
        return pltpu.make_async_remote_copy(
            src_ref=src, dst_ref=dst, send_sem=head_ssem.at[n], recv_sem=head_rsem.at[n],
            device_id=partner, device_id_type=pl.DeviceIdType.MESH,
        )

    enc_copy = head_copy(enc_send, enc_recv, 0)
    enc_copy.start()
    for u in range(USERS):
        limits = jnp.clip(cut_in[u : u + 1, :] - base, 0, EVENTS)
        limits = jnp.broadcast_to(limits, (DH, TARGETS)).T.reshape(NEAR, 2 * ROWS, DH)
        halves = [limits[:, n * ROWS : (n + 1) * ROWS, :].reshape(TARGETS // 2, DH) for n in range(2)]
        cut_v[u] = jnp.concatenate(halves, axis=0).T[: 2 * ROWS, :].astype(jnp.int16)
    cot = cot_v[...].astype(F32).reshape(OWN, MODEL).astype(BF)
    out_grad = contract_last(cot, wp_v[...]).astype(BF).astype(F32)
    enc_copy.wait()
    embedded = (0.5 * (enc_send[...] + enc_recv[...])).astype(BF)
    query_lin = dot(embedded, wq_v[...])
    queries = silu(query_lin).astype(BF).astype(F32)

    def send(src, dst, ssem, rsem, device):
        pltpu.make_async_remote_copy(
            src_ref=src, dst_ref=dst, send_sem=ssem, recv_sem=rsem,
            device_id=device, device_id_type=pl.DeviceIdType.MESH,
        ).start()

    def whole(ref, ssem, rsem):
        return pltpu.make_async_remote_copy(
            src_ref=ref, dst_ref=ref, send_sem=ssem, recv_sem=rsem,
            device_id=partner, device_id_type=pl.DeviceIdType.MESH,
        )

    def heads_stacked(rows):
        return jnp.concatenate([rows[:, :DH], rows[:, DH:]], axis=0)

    mine = ci * NEAR + spot
    near = pl.ds(ci * NEAR, NEAR)
    far = pl.ds((1 - ci) * NEAR, NEAR)

    def gather_sems(ph, u, n):
        return ag_ssem.at[ph, u, n], ag_rsem.at[ph, u, n]

    def gather_waits(ph, u):
        return (
            whole(ag.at[ph, u, 0 : NEAR - 1], *gather_sems(ph, u, 0)),
            whole(ag.at[ph, u, 0:NEAR], *gather_sems(ph, u, 1)),
        )

    def gather_first(ph, u, block):
        ag[ph, u, mine] = block
        ref = ag.at[ph, u, mine]
        for _, device in peers:
            send(ref, ref, *gather_sems(ph, u, 0), device)

    def gather_last(ph, u):
        gather_waits(ph, u)[0].wait_recv()
        ref = ag.at[ph, u, near]
        send(ref, ref, *gather_sems(ph, u, 1), sibling)

    def gather_end(ph, u):
        gather_waits(ph, u)[1].wait_recv()
        blocks = ag[ph, u].astype(F32)
        for h in range(2):
            rows = blocks[:, h * ROWS : (h + 1) * ROWS, :].reshape(TARGETS, DH)
            rows_v[h] = rows.astype(BF)

    def sum_sems(ph, u, n):
        return rs_ssem.at[ph, u, n], rs_rsem.at[ph, u, n]

    def sum_waits(ph, u):
        return (
            whole(rs1_recv.at[ph, u], *sum_sems(ph, u, 0)),
            whole(rs2_recv.at[ph, u, 0 : NEAR - 1], *sum_sems(ph, u, 1)),
        )

    def sum_first(ph, u):
        rs1_send[ph, u] = sums_v[...].astype(BF)
        send(rs1_send.at[ph, u, far], rs1_recv.at[ph, u], *sum_sems(ph, u, 0), sibling)

    def sum_mid(ph, u):
        sum_waits(ph, u)[0].wait_recv()
        total = rs1_send[ph, u, near].astype(F32) + rs1_recv[ph, u].astype(F32)
        rs2_send[ph, u] = total.astype(BF)
        rs2_recv[ph, u, spot] = rs2_send[ph, u, spot]
        for peer, device in peers:
            send(
                rs2_send.at[ph, u, peer], rs2_recv.at[ph, u, spot], *sum_sems(ph, u, 1), device
            )

    def sum_end(ph, u):
        sum_waits(ph, u)[1].wait_recv()
        return jnp.sum(rs2_recv[ph, u].astype(F32), axis=0)

    blocks = [heads_stacked(queries[u * ROWS : (u + 1) * ROWS]).astype(BF) for u in range(USERS)]
    for u in range(2):
        gather_first(0, u, blocks[u])
    lin_q[...] = silu_slope(query_lin)
    gate_lin = dot(embedded, wg_v[...])
    lin_g[...] = silu_slope(gate_lin)
    gates = silu(gate_lin).astype(BF).astype(F32)
    for u in range(USERS):
        gates_v[u] = heads_stacked(gates[u * ROWS : (u + 1) * ROWS])
        outg_v[u] = heads_stacked(out_grad[u * ROWS : (u + 1) * ROWS])
    gather_last(0, 0)
    for u in range(2, USERS):
        gather_first(0, u, blocks[u])
    gather_last(0, 1)

    def norm_and_gather(u):
        attended = sum_end(0, u)
        grads = outg_v[u]
        rscale = lax.rsqrt(jnp.mean(attended * attended, axis=-1, keepdims=True) + 1e-06)
        normed = attended * rscale
        gateg_v[u] = grads * normed
        ng = grads * gates_v[u]
        grad = rscale * (ng - normed * jnp.mean(ng * normed, axis=-1, keepdims=True))
        gather_first(1, u, grad.astype(BF))

    def query_grad_end(u):
        qgrad_v[u] = sum_end(1, u) * (0.5 * SCALE)

    def unstacked(ref, g):
        blocks = [ref[2 * g : 2 * g + 2, h * ROWS : (h + 1) * ROWS, :] for h in range(2)]
        return jnp.concatenate([block.reshape(GROUP, DH) for block in blocks], axis=1)

    def keep(h, sums):
        rows = pl.ds(pl.multiple_of(h * ROWS, ROWS), ROWS)
        sums_v[:, rows, :] = sums.T.reshape(SLOTS, ROWS, DH)

    def forward(u, h):
        cols = pl.ds(pl.multiple_of(h * DH, DH), DH)
        scores = contract_last(k_v[u, :, cols], rows_v[h])
        place = lax.broadcasted_iota(jnp.int32, (EVENTS, TARGETS), 0).astype(jnp.int16)
        visible = place < jnp.concatenate([cut_v[u]] * (EVENTS // (2 * ROWS)), axis=0)
        y = (scores * (0.5 * SCALE)).astype(BF)
        t = jnp.where(visible, jnp.tanh(y), BF(-1))
        s2 = BF(1) + t
        w = y * s2
        slope_v[u * 2 + h] = s2 + w * (BF(1) - t)
        keep(h, contract_first(v_v[u, :, cols], w))

    def backward(u, h):
        cols = pl.ds(pl.multiple_of(h * DH, DH), DH)
        wgrad = contract_last(v_v[u, :, cols], rows_v[h])
        gs = wgrad.astype(BF) * slope_v[u * 2 + h]
        keep(h, contract_first(k_v[u, :, cols], gs))

    @pl.loop(0, 4 * USERS)
    def _(i):
        u = lax.rem(i, 8) // 2
        h = lax.rem(i, 2)

        @pl.when(i < 8)
        def _():
            @pl.when(h == 0)
            def _():
                gather_end(0, u)
                for copy in kv_copies(u):
                    copy.wait()

            forward(u, h)

        @pl.when(i >= 8)
        def _():
            @pl.when(h == 0)
            def _():
                gather_end(1, u)

            backward(u, h)

        @pl.when(h == 1)
        def _():
            sum_first(i // 8, u)

        @pl.when((i == 6) | (i == 7) | (i == 8))
        def _():
            @pl.when(i == 7)
            def _():
                sum_mid(0, 3)

            norm_and_gather(i - 6 + i // 8)

        @pl.when((i == 2) | (i == 4) | (i == 6) | (i == 10) | (i == 12) | (i == 14))
        def _():
            sum_mid(i // 8, lax.rem(i, 8) // 2 - 1)

        @pl.when(i == 7)
        def _():
            gather_last(1, 0)
            norm_and_gather(2)

        @pl.when((i == 8) | (i == 10) | (i == 12))
        def _():
            gather_last(1, i // 2 - 3)

        @pl.when(i == 2)
        def _():
            gather_last(0, 2)
            gather_last(0, 3)

    sum_mid(1, USERS - 1)

    emb_copies, part_copies = [], []

    def embed_part(g):
        rows = slice(g * GROUP, (g + 1) * GROUP)
        for u in (2 * g, 2 * g + 1):
            query_grad_end(u)
        query_back = (unstacked(qgrad_v, g) * lin_q[rows, :]).astype(BF)
        gate_back = (unstacked(gateg_v, g) * lin_g[rows, :]).astype(BF)
        emb_send[g] = (
            contract_last(query_back, wq_v[...]) + contract_last(gate_back, wg_v[...])
        ).astype(BF)
        emb_copies.append(head_copy(emb_send.at[g], emb_recv.at[g], 1 + g))
        emb_copies[g].start()

    def content_part(g):
        emb_copies[g].wait()
        embed_grad = (0.5 * (emb_send[g].astype(F32) + emb_recv[g].astype(F32))).astype(BF)
        rows = slice(g * 64, (g + 1) * 64)
        spread_here = spread[rows, g * GROUP : (g + 1) * GROUP]
        hidden_grad = contract_last(dot(spread_here, embed_grad).astype(BF), we_v[...])
        x_v[rows, :] = (hidden_grad * hid_slope[rows, :]).astype(BF)
        other = pl.ds(pl.multiple_of((1 - hi) * 32, 32), 32)
        for j in range(OUT_CHUNKS):
            cols = slice(j * OUT_CHUNK, (j + 1) * OUT_CHUNK)
            part_own[g, :, cols] = contract_last(x_v[rows, :], wh_v[cols, :])
            part_send[g, j] = part_own[g, other, cols].astype(BF)
            n = g * OUT_CHUNKS + j
            part_copies.append(head_copy(part_send.at[g, j], part_recv.at[g, j], 3 + n))
            part_copies[n].start()

    def content_end(g):
        mine = pl.ds(pl.multiple_of(hi * 32, 32), 32)
        for j in range(OUT_CHUNKS):
            cols = slice(j * OUT_CHUNK, (j + 1) * OUT_CHUNK)
            part_copies[g * OUT_CHUNKS + j].wait()
            own = part_own[g, mine, cols].astype(BF).astype(F32)
            total = (own + part_recv[g, j].astype(F32)).astype(BF)
            out_ref[2 * g : 2 * g + 2, :, :, cols] = total.reshape(2, ROWS, 2, OUT_CHUNK)

    embed_part(0)
    content_part(0)
    embed_part(1)
    content_end(0)
    content_part(1)
    content_end(1)

    @pl.loop(0, USERS)
    def _(u):
        for ph in range(2):
            for copy in gather_waits(ph, u):
                copy.wait_send()
            for copy in sum_waits(ph, u):
                copy.wait_send()


def body(
    content_rows, w_hidden, w_embed, w_query, w_gate, w_proj,
    history_keys, history_values, cutoffs, out_cotangent,
):
    dma = pltpu.SemaphoreType.DMA
    v = pltpu.VMEM
    part = pl.pallas_call(
        kernel,
        name="attention_and_encoder",
        out_shape=jax.ShapeDtypeStruct((USERS, ROWS, 2, WIDTH), BF),
        in_specs=[pl.BlockSpec(memory_space=pl.ANY)] * 10,
        out_specs=pl.BlockSpec(memory_space=pltpu.VMEM),
        scratch_shapes=[
            v((USERS, ROWS, EACH, WIDTH), BF), v((USERS, TARGETS), jnp.int32), v((MODEL // DH, 64, DH), F32),
            v((EACH * OWN, WIDTH), BF), v((WIDTH, HALF), BF), v((HALF, MODEL), BF),
            v((MODEL, LOCAL), BF), v((MODEL, LOCAL), BF), v((LOCAL, MODEL), BF),
            v((USERS, EVENTS, LOCAL), BF), v((USERS, EVENTS, LOCAL), BF),
            v((USERS, 2 * ROWS, TARGETS), jnp.int16), v((USERS, ROWS, MODEL), BF),
            v((2 * USERS, EVENTS, TARGETS), BF), v((EACH * OWN, HALF), F32),
            v((OWN, MODEL), F32), v((OWN, MODEL), F32),
            v((OWN, LOCAL), F32), v((OWN, LOCAL), F32),
            v((USERS, 2 * ROWS, DH), F32), v((USERS, 2 * ROWS, DH), F32),
            v((USERS, 2 * ROWS, DH), F32), v((USERS, 2 * ROWS, DH), F32),
            v((2, USERS, SLOTS, 2 * ROWS, DH), BF), v((2, TARGETS, DH), BF),
            v((SLOTS, 2 * ROWS, DH), F32), v((2, USERS, SLOTS, 2 * ROWS, DH), BF),
            v((2, USERS, NEAR, 2 * ROWS, DH), BF), v((2, USERS, NEAR, 2 * ROWS, DH), BF),
            v((2, USERS, NEAR, 2 * ROWS, DH), BF),
            v((2, GROUP, MODEL), BF), v((2, GROUP, MODEL), BF),
            v((2, OUT_CHUNKS, 32, OUT_CHUNK), BF), v((2, OUT_CHUNKS, 32, OUT_CHUNK), BF),
            v((2, 64, WIDTH), F32),
            dma((7 + HID_CHUNKS,)), dma((2, USERS)),
            dma((2, USERS, 2)), dma((2, USERS, 2)), dma((2, USERS, 2)), dma((2, USERS, 2)),
            dma((3 + 2 * OUT_CHUNKS,)), dma((3 + 2 * OUT_CHUNKS,)),
        ],
        compiler_params=pltpu.CompilerParams(
            collective_id=0, has_side_effects=True, vmem_limit_bytes=62 * 2**20
        ),
    )(
        content_rows, w_hidden, w_embed, w_query, w_gate, w_proj,
        history_keys, history_values, cutoffs, out_cotangent,
    )
    return part


def solution(mesh):
    split = Mesh(
        mesh.devices.reshape(4, 4, 2, 2, mesh.shape["head"]),
        (*CTX, "head"),
    )
    return jax.shard_map(
        body,
        mesh=split,
        in_specs=(
            P(None, CTX, None, None), P(None, "head"), P("head", None), P(None, "head"),
            P(None, "head"), P("head", None), P(None, CTX, "head"), P(None, CTX, "head"),
            P(), P(None, CTX, None),
        ),
        out_specs=P(None, CTX, "head", None),
        check_vma=False,
    )
```

```python
import jax
import jax.numpy as jnp
from jax import lax
from jax.experimental import pallas as pl
from jax.experimental.pallas import tpu as pltpu
from jax.sharding import Mesh
from jax.sharding import PartitionSpec as P

DH = 128
CTX = ("x", "y", "zh", "c")
BF = jnp.bfloat16
F32 = jnp.float32
LAST = (((1,), (1,)), ((), ()))
USERS, ROWS, EACH, WIDTH = 4, 8, 4, 2048
HALF, MODEL, LOCAL = 2048, 512, 256
TARGETS, EVENTS = 512, 2304
OWN = USERS * ROWS
GROUP = 2 * ROWS
SLOTS, NEAR = 64, 32
OFFSETS = sorted(
    [(a, b, c) for a in range(4) for b in range(4) for c in range(2) if a or b or c],
    key=lambda t: -(min(t[0], 4 - t[0]) + min(t[1], 4 - t[1]) + 2 * t[2]),
)
HID_CHUNKS = 2
HID_CHUNK = HALF // HID_CHUNKS
OUT_CHUNKS = 4
OUT_CHUNK = WIDTH // OUT_CHUNKS
SCALE = DH**-0.5


def contract_last(left, right):
    return lax.dot_general(left, right, LAST, preferred_element_type=F32)


def contract_first(left, right):
    return lax.dot_general(left, right, (((0,), (0,)), ((), ())), preferred_element_type=F32)


def dot(left, right):
    return jnp.dot(left, right, preferred_element_type=F32)


def silu(v):
    return v * jax.nn.sigmoid(v)


def silu_slope(v):
    s = jax.nn.sigmoid(v)
    return s * (1.0 + v * (1.0 - s))


def kernel(
    x_hbm, wh_hbm, we_hbm, wq_hbm, wg_hbm, wp_hbm, k_hbm, v_hbm, cut_hbm, cot_hbm,
    out_ref,
    x_in, cut_in, pairs_v, x_v, wh_v, we_v, wq_v, wg_v, wp_v, k_v, v_v, cut_v, cot_v,
    slope_v, hid_slope, enc_send, enc_recv, lin_q, lin_g, gates_v, outg_v, gateg_v, qgrad_v,
    ag, rows_v, sums_v, rs1_send, rs1_recv, rs2_send, rs2_recv,
    emb_send, emb_recv, part_send, part_recv, part_own,
    load_sem, kv_sem, ag_ssem, ag_rsem, rs_ssem, rs_rsem, head_ssem, head_rsem,
):
    xi, yi, zi, ci, hi = (lax.axis_index(a) for a in (*CTX, "head"))
    base = (((xi * 4 + yi) * 2 + zi) * 2 + ci) * EVENTS
    partner = {"head": 1 - hi}
    sibling = {"c": 1 - ci}

    spot = (xi * 4 + yi) * 2 + zi
    peers = []
    for dx, dy, dz in OFFSETS:
        px, py, pz = lax.rem(xi + dx, 4), lax.rem(yi + dy, 4), lax.rem(zi + dz, 2)
        peers.append(((px * 4 + py) * 2 + pz, {"x": px, "y": py, "zh": pz}))

    barrier = pltpu.get_barrier_semaphore()
    for device in [partner, sibling] + [device for _, device in peers]:
        pl.semaphore_signal(barrier, inc=1, device_id=device, device_id_type=pl.DeviceIdType.MESH)

    loads = [pltpu.make_async_copy(x_hbm, x_in, load_sem.at[0])]
    for j in range(HID_CHUNKS):
        cols = pl.ds(j * HID_CHUNK, HID_CHUNK)
        loads.append(
            pltpu.make_async_copy(wh_hbm.at[:, cols], wh_v.at[:, cols], load_sem.at[len(loads)])
        )
    for src, dst in (
        (we_hbm, we_v), (cot_hbm, cot_v), (wp_hbm, wp_v), (wq_hbm, wq_v), (wg_hbm, wg_v),
        (cut_hbm, cut_in),
    ):
        loads.append(pltpu.make_async_copy(src, dst, load_sem.at[len(loads)]))
    for copy in loads:
        copy.start()

    def kv_copies(u):
        return (
            pltpu.make_async_copy(k_hbm.at[u], k_v.at[u], kv_sem.at[0, u]),
            pltpu.make_async_copy(v_hbm.at[u], v_v.at[u], kv_sem.at[1, u]),
        )

    row = lax.broadcasted_iota(jnp.int32, (EACH * OWN, EACH * OWN), 0)
    col = lax.broadcasted_iota(jnp.int32, (EACH * OWN, EACH * OWN), 1)
    target = (row // 64) * GROUP + (row % 32) // 2
    picked = col == target * EACH + ((row % 64) // 32) * 2 + row % 2
    order = jnp.where(picked, 1.0, 0.0).astype(BF)
    spread = jnp.where(target == col, 1.0, 0.0)[:, :OWN].astype(BF)
    loads[0].wait()
    x_v[...] = dot(order, x_in[...].reshape(EACH * OWN, WIDTH)).astype(BF)
    for j in range(HID_CHUNKS):
        loads[1 + j].wait()
        cols = slice(j * HID_CHUNK, (j + 1) * HID_CHUNK)
        lin = dot(x_v[...], wh_v[:, cols])
        s = jax.nn.sigmoid(lin)
        hidden = lin * s
        hid_slope[:, cols] = s * (1.0 + lin * (1.0 - s))
        if j == 0:
            loads[1 + HID_CHUNKS].wait()
        part = dot(hidden.astype(BF), we_v[cols, :])
        total = part if j == 0 else total + part
    for u in range(USERS):
        for copy in kv_copies(u):
            copy.start()
    for n in range(2 + HID_CHUNKS, 7 + HID_CHUNKS):
        loads[n].wait()
    pairs = jnp.concatenate([total[0:32] + total[32:64], total[64:96] + total[96:128]], axis=0)
    for n in range(MODEL // DH):
        cols = slice(n * DH, (n + 1) * DH)
        pairs_v[n] = pairs[:, cols]
        even, odd = (pairs_v[n, pl.ds(k, OWN, stride=2), :] for k in range(2))
        enc_send[:, cols] = even + odd

    pl.semaphore_wait(barrier, 33)

    def head_copy(src, dst, n):
        return pltpu.make_async_remote_copy(
            src_ref=src, dst_ref=dst, send_sem=head_ssem.at[n], recv_sem=head_rsem.at[n],
            device_id=partner, device_id_type=pl.DeviceIdType.MESH,
        )

    enc_copy = head_copy(enc_send, enc_recv, 0)
    enc_copy.start()
    for u in range(USERS):
        limits = jnp.clip(cut_in[u : u + 1, :] - base, 0, EVENTS)
        limits = jnp.broadcast_to(limits, (DH, TARGETS)).T.reshape(NEAR, 2 * ROWS, DH)
        halves = [limits[:, n * ROWS : (n + 1) * ROWS, :].reshape(TARGETS // 2, DH) for n in range(2)]
        cut_v[u] = jnp.concatenate(halves, axis=0).T[: 2 * ROWS, :].astype(jnp.int16)
    cot = cot_v[...].astype(F32).reshape(OWN, MODEL).astype(BF)
    out_grad = contract_last(cot, wp_v[...]).astype(BF).astype(F32)
    enc_copy.wait()
    embedded = (0.5 * (enc_send[...] + enc_recv[...])).astype(BF)
    query_lin = dot(embedded, wq_v[...])
    queries = silu(query_lin).astype(BF).astype(F32)

    def send(src, dst, ssem, rsem, device):
        pltpu.make_async_remote_copy(
            src_ref=src, dst_ref=dst, send_sem=ssem, recv_sem=rsem,
            device_id=device, device_id_type=pl.DeviceIdType.MESH,
        ).start()

    def whole(ref, ssem, rsem):
        return pltpu.make_async_remote_copy(
            src_ref=ref, dst_ref=ref, send_sem=ssem, recv_sem=rsem,
            device_id=partner, device_id_type=pl.DeviceIdType.MESH,
        )

    def heads_stacked(rows):
        return jnp.concatenate([rows[:, :DH], rows[:, DH:]], axis=0)

    mine = ci * NEAR + spot
    near = pl.ds(ci * NEAR, NEAR)
    far = pl.ds((1 - ci) * NEAR, NEAR)

    def gather_sems(ph, u, n):
        return ag_ssem.at[ph, u, n], ag_rsem.at[ph, u, n]

    def gather_waits(ph, u):
        return (
            whole(ag.at[ph, u, 0 : NEAR - 1], *gather_sems(ph, u, 0)),
            whole(ag.at[ph, u, 0:NEAR], *gather_sems(ph, u, 1)),
        )

    def gather_first(ph, u, block):
        ag[ph, u, mine] = block
        ref = ag.at[ph, u, mine]
        for _, device in peers:
            send(ref, ref, *gather_sems(ph, u, 0), device)

    def gather_last(ph, u):
        gather_waits(ph, u)[0].wait_recv()
        ref = ag.at[ph, u, near]
        send(ref, ref, *gather_sems(ph, u, 1), sibling)

    def gather_end(ph, u):
        gather_waits(ph, u)[1].wait_recv()
        blocks = ag[ph, u].astype(F32)
        for h in range(2):
            rows = blocks[:, h * ROWS : (h + 1) * ROWS, :].reshape(TARGETS, DH)
            rows_v[h] = rows.astype(BF)

    def sum_sems(ph, u, n):
        return rs_ssem.at[ph, u, n], rs_rsem.at[ph, u, n]

    def sum_waits(ph, u):
        return (
            whole(rs1_recv.at[ph, u], *sum_sems(ph, u, 0)),
            whole(rs2_recv.at[ph, u, 0 : NEAR - 1], *sum_sems(ph, u, 1)),
        )

    def sum_first(ph, u):
        rs1_send[ph, u] = sums_v[...].astype(BF)
        send(rs1_send.at[ph, u, far], rs1_recv.at[ph, u], *sum_sems(ph, u, 0), sibling)

    def sum_mid(ph, u):
        sum_waits(ph, u)[0].wait_recv()
        total = rs1_send[ph, u, near].astype(F32) + rs1_recv[ph, u].astype(F32)
        rs2_send[ph, u] = total.astype(BF)
        rs2_recv[ph, u, spot] = rs2_send[ph, u, spot]
        for peer, device in peers:
            send(
                rs2_send.at[ph, u, peer], rs2_recv.at[ph, u, spot], *sum_sems(ph, u, 1), device
            )

    def sum_end(ph, u):
        sum_waits(ph, u)[1].wait_recv()
        return jnp.sum(rs2_recv[ph, u].astype(F32), axis=0)

    blocks = [heads_stacked(queries[u * ROWS : (u + 1) * ROWS]).astype(BF) for u in range(USERS)]
    for u in range(2):
        gather_first(0, u, blocks[u])
    lin_q[...] = silu_slope(query_lin)
    gate_lin = dot(embedded, wg_v[...])
    lin_g[...] = silu_slope(gate_lin)
    gates = silu(gate_lin).astype(BF).astype(F32)
    for u in range(USERS):
        gates_v[u] = heads_stacked(gates[u * ROWS : (u + 1) * ROWS])
        outg_v[u] = heads_stacked(out_grad[u * ROWS : (u + 1) * ROWS])
    gather_last(0, 0)
    for u in range(2, USERS):
        gather_first(0, u, blocks[u])
    gather_last(0, 1)

    def norm_and_gather(u):
        attended = sum_end(0, u)
        grads = outg_v[u]
        rscale = lax.rsqrt(jnp.mean(attended * attended, axis=-1, keepdims=True) + 1e-06)
        normed = attended * rscale
        gateg_v[u] = grads * normed
        ng = grads * gates_v[u]
        grad = rscale * (ng - normed * jnp.mean(ng * normed, axis=-1, keepdims=True))
        gather_first(1, u, grad.astype(BF))

    def query_grad_end(u):
        qgrad_v[u] = sum_end(1, u) * (0.5 * SCALE)

    def unstacked(ref, g):
        blocks = [ref[2 * g : 2 * g + 2, h * ROWS : (h + 1) * ROWS, :] for h in range(2)]
        return jnp.concatenate([block.reshape(GROUP, DH) for block in blocks], axis=1)

    def keep(h, sums):
        rows = pl.ds(pl.multiple_of(h * ROWS, ROWS), ROWS)
        sums_v[:, rows, :] = sums.T.reshape(SLOTS, ROWS, DH)

    def forward(u, h):
        cols = pl.ds(pl.multiple_of(h * DH, DH), DH)
        scores = contract_last(k_v[u, :, cols], rows_v[h])
        place = lax.broadcasted_iota(jnp.int32, (EVENTS, TARGETS), 0).astype(jnp.int16)
        visible = place < jnp.concatenate([cut_v[u]] * (EVENTS // (2 * ROWS)), axis=0)
        y = (scores * (0.5 * SCALE)).astype(BF)
        t = jnp.where(visible, jnp.tanh(y), BF(-1))
        s2 = BF(1) + t
        w = y * s2
        slope_v[u * 2 + h] = s2 + w * (BF(1) - t)
        keep(h, contract_first(v_v[u, :, cols], w))

    def backward(u, h):
        cols = pl.ds(pl.multiple_of(h * DH, DH), DH)
        wgrad = contract_last(v_v[u, :, cols], rows_v[h])
        gs = wgrad.astype(BF) * slope_v[u * 2 + h]
        keep(h, contract_first(k_v[u, :, cols], gs))

    @pl.loop(0, 4 * USERS)
    def _(i):
        u = lax.rem(i, 8) // 2
        h = lax.rem(i, 2)

        @pl.when(i < 8)
        def _():
            @pl.when(h == 0)
            def _():
                gather_end(0, u)
                for copy in kv_copies(u):
                    copy.wait()

            forward(u, h)

        @pl.when(i >= 8)
        def _():
            @pl.when(h == 0)
            def _():
                gather_end(1, u)

            backward(u, h)

        @pl.when(h == 1)
        def _():
            sum_first(i // 8, u)

        @pl.when((i == 6) | (i == 7) | (i == 8))
        def _():
            @pl.when(i == 7)
            def _():
                sum_mid(0, 3)

            norm_and_gather(i - 6 + i // 8)

        @pl.when((i == 2) | (i == 4) | (i == 6) | (i == 10) | (i == 12) | (i == 14))
        def _():
            sum_mid(i // 8, lax.rem(i, 8) // 2 - 1)

        @pl.when(i == 7)
        def _():
            gather_last(1, 0)
            norm_and_gather(2)

        @pl.when((i == 8) | (i == 10) | (i == 12))
        def _():
            gather_last(1, i // 2 - 3)

        @pl.when(i == 2)
        def _():
            gather_last(0, 2)
            gather_last(0, 3)

    sum_mid(1, USERS - 1)

    emb_copies, part_copies = [], []

    def embed_part(g):
        rows = slice(g * GROUP, (g + 1) * GROUP)
        for u in (2 * g, 2 * g + 1):
            query_grad_end(u)
        query_back = (unstacked(qgrad_v, g) * lin_q[rows, :]).astype(BF)
        gate_back = (unstacked(gateg_v, g) * lin_g[rows, :]).astype(BF)
        emb_send[g] = (
            contract_last(query_back, wq_v[...]) + contract_last(gate_back, wg_v[...])
        ).astype(BF)
        emb_copies.append(head_copy(emb_send.at[g], emb_recv.at[g], 1 + g))
        emb_copies[g].start()

    def content_part(g):
        emb_copies[g].wait()
        embed_grad = (0.5 * (emb_send[g].astype(F32) + emb_recv[g].astype(F32))).astype(BF)
        rows = slice(g * 64, (g + 1) * 64)
        spread_here = spread[rows, g * GROUP : (g + 1) * GROUP]
        hidden_grad = contract_last(dot(spread_here, embed_grad).astype(BF), we_v[...])
        x_v[rows, :] = (hidden_grad * hid_slope[rows, :]).astype(BF)
        other = pl.ds(pl.multiple_of((1 - hi) * 32, 32), 32)
        for j in range(OUT_CHUNKS):
            cols = slice(j * OUT_CHUNK, (j + 1) * OUT_CHUNK)
            part_own[g, :, cols] = contract_last(x_v[rows, :], wh_v[cols, :])
            part_send[g, j] = part_own[g, other, cols].astype(BF)
            n = g * OUT_CHUNKS + j
            part_copies.append(head_copy(part_send.at[g, j], part_recv.at[g, j], 3 + n))
            part_copies[n].start()

    def content_end(g):
        mine = pl.ds(pl.multiple_of(hi * 32, 32), 32)
        for j in range(OUT_CHUNKS):
            cols = slice(j * OUT_CHUNK, (j + 1) * OUT_CHUNK)
            part_copies[g * OUT_CHUNKS + j].wait()
            own = part_own[g, mine, cols].astype(BF).astype(F32)
            total = (own + part_recv[g, j].astype(F32)).astype(BF)
            out_ref[2 * g : 2 * g + 2, :, :, cols] = total.reshape(2, ROWS, 2, OUT_CHUNK)

    embed_part(0)
    content_part(0)
    embed_part(1)
    content_end(0)
    content_part(1)
    content_end(1)

    @pl.loop(0, USERS)
    def _(u):
        for ph in range(2):
            for copy in gather_waits(ph, u):
                copy.wait_send()
            for copy in sum_waits(ph, u):
                copy.wait_send()


def body(
    content_rows, w_hidden, w_embed, w_query, w_gate, w_proj,
    history_keys, history_values, cutoffs, out_cotangent,
):
    dma = pltpu.SemaphoreType.DMA
    v = pltpu.VMEM
    part = pl.pallas_call(
        kernel,
        name="attention_and_encoder",
        out_shape=jax.ShapeDtypeStruct((USERS, ROWS, 2, WIDTH), BF),
        in_specs=[pl.BlockSpec(memory_space=pl.ANY)] * 10,
        out_specs=pl.BlockSpec(memory_space=pltpu.VMEM),
        scratch_shapes=[
            v((USERS, ROWS, EACH, WIDTH), BF), v((USERS, TARGETS), jnp.int32), v((MODEL // DH, 64, DH), F32),
            v((EACH * OWN, WIDTH), BF), v((WIDTH, HALF), BF), v((HALF, MODEL), BF),
            v((MODEL, LOCAL), BF), v((MODEL, LOCAL), BF), v((LOCAL, MODEL), BF),
            v((USERS, EVENTS, LOCAL), BF), v((USERS, EVENTS, LOCAL), BF),
            v((USERS, 2 * ROWS, TARGETS), jnp.int16), v((USERS, ROWS, MODEL), BF),
            v((2 * USERS, EVENTS, TARGETS), BF), v((EACH * OWN, HALF), F32),
            v((OWN, MODEL), F32), v((OWN, MODEL), F32),
            v((OWN, LOCAL), F32), v((OWN, LOCAL), F32),
            v((USERS, 2 * ROWS, DH), F32), v((USERS, 2 * ROWS, DH), F32),
            v((USERS, 2 * ROWS, DH), F32), v((USERS, 2 * ROWS, DH), F32),
            v((2, USERS, SLOTS, 2 * ROWS, DH), BF), v((2, TARGETS, DH), BF),
            v((SLOTS, 2 * ROWS, DH), F32), v((2, USERS, SLOTS, 2 * ROWS, DH), BF),
            v((2, USERS, NEAR, 2 * ROWS, DH), BF), v((2, USERS, NEAR, 2 * ROWS, DH), BF),
            v((2, USERS, NEAR, 2 * ROWS, DH), BF),
            v((2, GROUP, MODEL), BF), v((2, GROUP, MODEL), BF),
            v((2, OUT_CHUNKS, 32, OUT_CHUNK), BF), v((2, OUT_CHUNKS, 32, OUT_CHUNK), BF),
            v((2, 64, WIDTH), F32),
            dma((7 + HID_CHUNKS,)), dma((2, USERS)),
            dma((2, USERS, 2)), dma((2, USERS, 2)), dma((2, USERS, 2)), dma((2, USERS, 2)),
            dma((3 + 2 * OUT_CHUNKS,)), dma((3 + 2 * OUT_CHUNKS,)),
        ],
        compiler_params=pltpu.CompilerParams(
            collective_id=0, has_side_effects=True, vmem_limit_bytes=62 * 2**20
        ),
    )(
        content_rows, w_hidden, w_embed, w_query, w_gate, w_proj,
        history_keys, history_values, cutoffs, out_cotangent,
    )
    return part


def solution(mesh):
    split = Mesh(
        mesh.devices.reshape(4, 4, 2, 2, mesh.shape["head"]),
        (*CTX, "head"),
    )
    return jax.shard_map(
        body,
        mesh=split,
        in_specs=(
            P(None, CTX, None, None), P(None, "head"), P("head", None), P(None, "head"),
            P(None, "head"), P("head", None), P(None, CTX, "head"), P(None, CTX, "head"),
            P(), P(None, CTX, None),
        ),
        out_specs=P(None, CTX, "head", None),
        check_vma=False,
    )
```
